512 devices in a mesh: dp: 64 (over z, y), tensor: 8 (over x, core).
Axes of the slice: x: 4, y: 4, z: 16, core: 2. Of those that a mesh axis runs over, the one named last changes fastest.
Arguments:
- grads: bfloat16 [131072, 3072], P('dp', 'tensor'), may hold values from -16 to 16, as said below
- errors: bfloat16 [131072, 3072], P('dp', 'tensor'), may hold values from -4 to 4
- q_init: float32 [3072, 128], P('tensor'), may hold values from -6 to 6
Outputs:
- avg_grad: bfloat16 [2048, 3072], P('dp', 'tensor')
- new_errors: bfloat16 [131072, 3072], P('dp', 'tensor')
- q_next: float32 [3072, 128], P('tensor')
The draws below stay inside these ranges and needn't reach their ends.
Inputs may be any that keep to these rules, and one draw needn't show every extreme that they name: `grads`: gradients of the 64 replicas, stacked along rows.
All inputs are finite; a program needn't handle non-finite values.
Results may differ from the reference program's by a relative error of at most 0.0035.
Values sent between devices are 32-bit elements; how exact they have to be, the bound alone decides.
No kernel may reach another device: no remote copies, remote signals or barrier semaphores. Data moves between devices by JAX's collectives and lax.ppermute only.
A program may use at most 64 MiB of HBM per device.

```python
import math
import jax
import jax.numpy as jnp
from jax import lax

ROWS = 2048
COLS = 3072
RANK = 128
GROWS = 131072
N_DP = 64


def draw_grads(key, part):
    key = jax.random.fold_in(key, 11)
    key_common, key_noise, key_scale = jax.random.split(key, 3)
    position = jnp.arange(ROWS, dtype=jnp.float32) / ROWS
    trend = jnp.exp(math.log(3.0) * position)
    spread = jnp.exp(jax.random.uniform(key_scale, (ROWS,), jnp.float32, 0.0, math.log(10.0)))
    common = jax.random.normal(key_common, (ROWS, COLS), jnp.float32)
    noise = 0.7 * jax.random.normal(key_noise, (N_DP, ROWS, COLS), jnp.float32)
    factor = trend * spread / 4.0
    values = factor[None, :, None] * (common[None] + noise)
    values = jnp.clip(values, -16.0, 16.0)
    return values.reshape(N_DP * ROWS, COLS).astype(jnp.bfloat16)


def block_scale(own_key, extent, pieces, least, largest):
    level, own = 1.0, jax.random.fold_in(own_key, 6)
    for dim, parts in pieces:
        heights = jnp.exp(jax.random.uniform(jax.random.fold_in(own, dim), (parts,), jnp.float32, least / len(pieces), largest / len(pieces)))
        level = level * jnp.repeat(heights, extent[dim] // parts).reshape([-1 if axis == dim else 1 for axis in range(len(extent))])
    return level


def centred(stream_key, extent, scale, bound, pieces=(), kind=jnp.bfloat16):
    entries = jax.random.normal(stream_key, extent, jnp.float32) * scale
    if len(pieces) > 0:
        entries = block_scale(stream_key, extent, pieces, -0.22, 0.18) * entries
    return jnp.clip(entries, min=-bound, max=bound).astype(kind)


def setup_inputs(seed: int = 0) -> dict:
    splits = jax.random.split(jax.random.key(seed), 4)
    return {
        "grads": draw_grads(jax.random.fold_in(splits[3], 71), 0),
        "errors": centred(splits[1], (GROWS, COLS), 0.5, 4.0, ((0, 64), (1, 8))),
        "q_init": centred(splits[2], (COLS, RANK), 1.0, 6.0, ((0, 8),), jnp.float32),
    }


def cholesky_qr(values):
    for sweep in range(2):
        gram_local = jnp.dot(values.T, values, precision=lax.Precision.HIGHEST)
        lower = jnp.linalg.cholesky(gram_local)
        values = jax.scipy.linalg.solve_triangular(lower, values.T, lower=True).T
    return values

def reference(grads, errors, q_init):
    merged = grads.astype(jnp.float32) + errors.astype(jnp.float32)
    summed = merged.reshape(N_DP, ROWS, COLS).sum(axis=0)
    power_part = jnp.dot(summed, q_init, precision=lax.Precision.HIGHEST)
    ortho_basis = cholesky_qr(power_part)
    factor_q = jnp.dot(summed.T, ortho_basis, precision=lax.Precision.HIGHEST) * (1.0 / N_DP)
    approx = jnp.dot(ortho_basis, factor_q.T, precision=lax.Precision.HIGHEST)
    new_errors = (merged.reshape(N_DP, ROWS, COLS) - approx[None]).reshape(N_DP * ROWS, COLS)
    return (approx.astype(jnp.bfloat16), new_errors.astype(jnp.bfloat16), factor_q)
```

```python
import functools

import jax
import jax.numpy as jnp
from jax import lax
from jax.experimental import pallas as pl
from jax.experimental.pallas import tpu as pltpu
from jax.sharding import Mesh, PartitionSpec as P

F32 = jnp.float32
BF16 = jnp.bfloat16
HIGHEST = lax.Precision.HIGHEST
ROWS_BY_ROWS = (((0,), (0,)), ((), ()))
LANES_BY_LANES = (((1,), (1,)), ((), ()))
WIDTH = 8
TILE = 512
VMEM_BYTES = 40 << 20

DP = ("far", "near", "y")
TENSOR = ("x", "core")


def pieces(values, count):
    parts = []
    for _ in range(count):
        part = values.astype(BF16)
        parts.append(part)
        values = values - part.astype(F32)
    return parts


def whole(ref_shape):
    return pl.BlockSpec(ref_shape, lambda *_: (0,) * len(ref_shape))


def power_kernel(grads_ref, errors_ref, q_ref, power_ref, split_ref):
    rank = q_ref.shape[1]

    @pl.when(pl.program_id(0) == 0)
    def _():
        for k, part in enumerate(pieces(q_ref[...], 3)):
            split_ref[:, k * rank : (k + 1) * rank] = part

    products = jnp.dot(grads_ref[...], split_ref[...], preferred_element_type=F32)
    products += jnp.dot(errors_ref[...], split_ref[...], preferred_element_type=F32)
    power_ref[...] = products[:, :rank] + (products[:, rank : 2 * rank] + products[:, 2 * rank :])


def power_terms(grads, errors, q_init):
    rows, cols = grads.shape
    rank = q_init.shape[1]
    tiled = pl.BlockSpec((TILE, cols), lambda i: (i, 0))
    return pl.pallas_call(
        power_kernel,
        grid=(rows // TILE,),
        out_shape=jax.ShapeDtypeStruct((rows, rank), F32),
        in_specs=[tiled, tiled, whole((cols, rank))],
        out_specs=pl.BlockSpec((TILE, rank), lambda i: (i, 0)),
        scratch_shapes=[pltpu.VMEM((cols, 3 * rank), BF16)],
        compiler_params=pltpu.CompilerParams(vmem_limit_bytes=VMEM_BYTES),
    )(grads, errors, q_init)


def inverse_factor(gram, work_ref, inverse_ref):
    rank = gram.shape[0]
    lanes = lax.broadcasted_iota(jnp.int32, (WIDTH, rank), 1)
    subs = lax.broadcasted_iota(jnp.int32, (WIDTH, rank), 0)
    spread = lambda row: jnp.broadcast_to(row, (WIDTH, rank))
    work_ref[...] = gram
    for low in range(0, rank, WIDTH):
        own = work_ref[low : low + WIDTH, :]
        inside = (lanes >= low) & (lanes < low + WIDTH)
        columns = [spread(own[:, low + k : low + k + 1]) for k in range(WIDTH)]
        block = jnp.where(inside, (lanes - low == subs).astype(F32), own)
        forward = jnp.zeros((WIDTH, rank), F32)
        pivots = jnp.ones((WIDTH, rank), F32)
        reciprocals = jnp.zeros((WIDTH, rank), F32)
        for j in range(WIDTH):
            heads = [spread(column[j : j + 1, :]) for column in columns[j:]]
            row = spread(block[j : j + 1, :])
            forward = jnp.where(subs == j, row, forward)
            pivots = jnp.where(subs == j, heads[0], pivots)
            reciprocal = 1.0 / heads[0]
            reciprocals = jnp.where(subs == j, reciprocal, reciprocals)
            factor = jnp.where(subs == j, 0.0, columns[j] * reciprocal)
            for k in range(j + 1, WIDTH):
                columns[k] = columns[k] - factor * heads[k - j]
            block = block - factor * row
        inverse_ref[low : low + WIDTH, :] = jnp.where(lanes < low + WIDTH, forward * lax.rsqrt(pivots), 0.0)
        block = block * reciprocals
        solved = [spread(block[k : k + 1, :]) for k in range(WIDTH)]
        for at in range(low + WIDTH, rank, WIDTH):
            rest = work_ref[at : at + WIDTH, :]
            terms = [spread(rest[:, low + k : low + k + 1]) * solved[k] for k in range(WIDTH)]
            while len(terms) > 1:
                terms = [a + b for a, b in zip(terms[::2], terms[1::2], strict=True)]
            work_ref[at : at + WIDTH, :] = jnp.where(inside, 0.0, rest) - terms[0]


def basis_kernel(power_ref, basis_ref, inverse_ref, work_ref, step_ref):
    first = None
    source = power_ref
    for _ in range(2):
        gram = lax.dot_general(source[...], source[...], ROWS_BY_ROWS, precision=HIGHEST, preferred_element_type=F32)
        inverse_factor(gram, work_ref, step_ref)
        step = step_ref[...]
        basis_ref[...] = lax.dot_general(source[...], step, LANES_BY_LANES, precision=HIGHEST, preferred_element_type=F32)
        source = basis_ref
        first = step if first is None else jnp.dot(step, first, precision=HIGHEST, preferred_element_type=F32)
    inverse_ref[...] = first


def basis_of(power):
    rows, rank = power.shape
    in_vmem = pl.BlockSpec(memory_space=pltpu.VMEM)
    return pl.pallas_call(
        basis_kernel,
        out_shape=(jax.ShapeDtypeStruct((rows, rank), F32), jax.ShapeDtypeStruct((rank, rank), F32)),
        in_specs=[in_vmem],
        out_specs=(in_vmem, in_vmem),
        scratch_shapes=[pltpu.VMEM((rank, rank), F32)] * 2,
        compiler_params=pltpu.CompilerParams(vmem_limit_bytes=VMEM_BYTES),
    )(power)


def factor_kernel(grads_ref, errors_ref, power_ref, terms_ref, sum_ref):
    rank = power_ref.shape[1]
    split = jnp.concatenate(pieces(power_ref[...], 2), axis=1)
    products = lax.dot_general(split, grads_ref[...], ROWS_BY_ROWS, preferred_element_type=F32)
    products += lax.dot_general(split, errors_ref[...], ROWS_BY_ROWS, preferred_element_type=F32)

    @pl.when(pl.program_id(0) == 0)
    def _():
        sum_ref[...] = products

    @pl.when(pl.program_id(0) > 0)
    def _():
        sum_ref[...] += products

    terms_ref[...] = sum_ref[:rank, :] + sum_ref[rank:, :]


def factor_terms(grads, errors, power):
    rows, cols = grads.shape
    rank = power.shape[1]
    tiled = pl.BlockSpec((TILE, cols), lambda i: (i, 0))
    return pl.pallas_call(
        factor_kernel,
        grid=(rows // TILE,),
        out_shape=jax.ShapeDtypeStruct((rank, cols), F32),
        in_specs=[tiled, tiled, pl.BlockSpec((TILE, rank), lambda i: (i, 0))],
        out_specs=whole((rank, cols)),
        scratch_shapes=[pltpu.VMEM((2 * rank, cols), F32)],
        compiler_params=pltpu.CompilerParams(vmem_limit_bytes=VMEM_BYTES),
    )(grads, errors, power)


def output_kernel(replicas, own_ref, grads_ref, errors_ref, basis_ref, share_ref, inverse_ref, terms_ref,
                  avg_ref, new_ref, q_ref, split_ref):
    def decompressed(rows):
        high, low = pieces(rows, 2)
        return jnp.dot(jnp.concatenate([high, high, low], axis=1), split_ref[...], preferred_element_type=F32)

    @pl.when(pl.program_id(0) == 0)
    def _():
        factor = jnp.dot(inverse_ref[...], terms_ref[...], precision=HIGHEST, preferred_element_type=F32)
        factor = factor * (1.0 / replicas)
        q_ref[...] = factor.T
        high, low = pieces(factor, 2)
        split_ref[...] = jnp.concatenate([high, low, high], axis=0)
        avg_ref[...] = decompressed(share_ref[...]).astype(BF16)

    merged = grads_ref[...].astype(F32) + errors_ref[...].astype(F32)
    new_ref[...] = (merged - decompressed(basis_ref[...])).astype(BF16)


def outputs(grads, errors, basis, inverse, terms, replicas, own):
    rows, cols = grads.shape
    rank = basis.shape[1]
    share = rows // replicas
    tiled = pl.BlockSpec((TILE, cols), lambda i, own: (i, 0))
    return pl.pallas_call(
        functools.partial(output_kernel, replicas),
        grid_spec=pltpu.PrefetchScalarGridSpec(
            num_scalar_prefetch=1,
            grid=(rows // TILE,),
            in_specs=[
                tiled,
                tiled,
                pl.BlockSpec((TILE, rank), lambda i, own: (i, 0)),
                pl.BlockSpec((share, rank), lambda i, own: (own[0], 0)),
                whole((rank, rank)),
                whole((rank, cols)),
            ],
            out_specs=(whole((share, cols)), tiled, whole((cols, rank))),
            scratch_shapes=[pltpu.VMEM((3 * rank, cols), BF16)],
        ),
        out_shape=(
            jax.ShapeDtypeStruct((share, cols), BF16),
            jax.ShapeDtypeStruct((rows, cols), BF16),
            jax.ShapeDtypeStruct((cols, rank), F32),
        ),
        compiler_params=pltpu.CompilerParams(vmem_limit_bytes=VMEM_BYTES),
    )(own, grads, errors, basis, basis, inverse, terms)


def scatter_sum(values, axes):
    count = lax.axis_size(axes)
    shares = lax.all_to_all(values, axes, 0, 0, tiled=True)
    return shares.reshape(count, values.shape[0] // count, values.shape[1]).sum(axis=0)


def gather(values, axes):
    count = lax.axis_size(axes)
    copies = jnp.broadcast_to(values[None], (count, *values.shape)).reshape(-1, values.shape[1])
    return lax.all_to_all(copies, axes, 0, 0, tiled=True)


def exchange_sum(values, axes):
    return gather(values, axes).reshape(lax.axis_size(axes), *values.shape).sum(axis=0)


def body(grads, errors, q_init):
    replicas = lax.axis_size(DP)
    power = power_terms(grads, errors, q_init)
    power = scatter_sum(power, "core")
    power = scatter_sum(power, ("y", "x"))
    power = exchange_sum(power, "near")
    power = exchange_sum(power, "far")
    power = gather(power, ("y", "x"))
    power = gather(power, "core")

    terms = factor_terms(grads, errors, power)
    terms = scatter_sum(terms, ("near", "y"))
    terms = exchange_sum(terms, "far")
    terms = gather(terms, ("near", "y"))

    basis, inverse = basis_of(power)
    own = lax.axis_index(DP).reshape(1)
    return outputs(grads, errors, basis, inverse, terms, replicas, own)


def solution(mesh):
    near = 4
    fine = Mesh(mesh.devices.reshape(4, near, 4, 4, 2), ("far", "near", "y", "x", "core"))
    placed = (P(DP, TENSOR), P(DP, TENSOR), P(TENSOR, None))
    return jax.shard_map(
        body,
        mesh=fine,
        in_specs=placed,
        out_specs=(P(DP, TENSOR), P(DP, TENSOR), P(TENSOR, None)),
        check_vma=False,
    )
```

```python
import functools

import jax
import jax.numpy as jnp
from jax import lax
from jax.experimental import pallas as pl
from jax.experimental.pallas import tpu as pltpu
from jax.sharding import Mesh, PartitionSpec as P

F32 = jnp.float32
BF16 = jnp.bfloat16
HIGHEST = lax.Precision.HIGHEST
ROWS_BY_ROWS = (((0,), (0,)), ((), ()))
LANES_BY_LANES = (((1,), (1,)), ((), ()))
WIDTH = 8
TILE = 512
VMEM_BYTES = 32 << 20
POWER_VMEM_BYTES = 60 << 20
OUTPUT_VMEM_BYTES = 52 << 20
QR_COST = pl.CostEstimate(flops=7_000_000_000, bytes_accessed=1 << 20, transcendentals=0)

DP = ("far", "near", "y")
TENSOR = ("x", "core")


def pieces(values, count):
    parts = []
    for _ in range(count):
        part = values.astype(BF16)
        parts.append(part)
        values = values - part.astype(F32)
    return parts


def whole(ref_shape):
    return pl.BlockSpec(ref_shape, lambda *_: (0,) * len(ref_shape))


def power_kernel(grads_ref, errors_ref, q_ref, power_ref, split_ref):
    rank = q_ref.shape[1]

    @pl.when(pl.program_id(0) == 0)
    def _():
        for k, part in enumerate(pieces(q_ref[...], 3)):
            split_ref[:, k * rank : (k + 1) * rank] = part

    products = jnp.dot(grads_ref[...], split_ref[...], preferred_element_type=F32)
    products += jnp.dot(errors_ref[...], split_ref[...], preferred_element_type=F32)
    power_ref[...] = products[:, :rank] + (products[:, rank : 2 * rank] + products[:, 2 * rank :])


def power_terms(grads, errors, q_init):
    rows, cols = grads.shape
    rank = q_init.shape[1]
    tiled = pl.BlockSpec((TILE, cols), lambda i: (i, 0))
    return pl.pallas_call(
        power_kernel,
        grid=(rows // TILE,),
        out_shape=jax.ShapeDtypeStruct((rows, rank), F32),
        in_specs=[tiled, tiled, whole((cols, rank))],
        out_specs=pl.BlockSpec((TILE, rank), lambda i: (i, 0)),
        scratch_shapes=[pltpu.VMEM((cols, 3 * rank), BF16)],
        compiler_params=pltpu.CompilerParams(vmem_limit_bytes=POWER_VMEM_BYTES),
    )(grads, errors, q_init)


def inverse_factor(gram, work_ref, inverse_ref):
    rank = gram.shape[0]
    lanes = lax.broadcasted_iota(jnp.int32, (WIDTH, rank), 1)
    subs = lax.broadcasted_iota(jnp.int32, (WIDTH, rank), 0)
    spread = lambda row: jnp.broadcast_to(row, (WIDTH, rank))
    work_ref[...] = gram
    for low in range(0, rank, WIDTH):
        own = work_ref[low : low + WIDTH, :]
        inside = (lanes >= low) & (lanes < low + WIDTH)
        columns = [spread(own[:, low + k : low + k + 1]) for k in range(WIDTH)]
        block = jnp.where(inside, (lanes - low == subs).astype(F32), own)
        forward = jnp.zeros((WIDTH, rank), F32)
        pivots = jnp.ones((WIDTH, rank), F32)
        reciprocals = jnp.zeros((WIDTH, rank), F32)
        for j in range(WIDTH):
            heads = [spread(column[j : j + 1, :]) for column in columns[j:]]
            row = spread(block[j : j + 1, :])
            forward = jnp.where(subs == j, row, forward)
            pivots = jnp.where(subs == j, heads[0], pivots)
            reciprocal = 1.0 / heads[0]
            reciprocals = jnp.where(subs == j, reciprocal, reciprocals)
            factor = jnp.where(subs == j, 0.0, columns[j] * reciprocal)
            for k in range(j + 1, WIDTH):
                columns[k] = columns[k] - factor * heads[k - j]
            block = block - factor * row
        inverse_ref[low : low + WIDTH, :] = jnp.where(lanes < low + WIDTH, forward * lax.rsqrt(pivots), 0.0)
        block = block * reciprocals
        solved = [spread(block[k : k + 1, :]) for k in range(WIDTH)]
        for at in range(low + WIDTH, rank, WIDTH):
            rest = work_ref[at : at + WIDTH, :]
            terms = [spread(rest[:, low + k : low + k + 1]) * solved[k] for k in range(WIDTH)]
            while len(terms) > 1:
                terms = [a + b for a, b in zip(terms[::2], terms[1::2], strict=True)]
            work_ref[at : at + WIDTH, :] = jnp.where(inside, 0.0, rest) - terms[0]


def first_pass_kernel(power_ref, first_ref, work_ref):
    power = power_ref[...]
    gram = lax.dot_general(power, power, ROWS_BY_ROWS, precision=HIGHEST, preferred_element_type=F32)
    inverse_factor(gram, work_ref, first_ref)


def second_pass_kernel(power_ref, first_ref, maps_ref, work_ref, second_ref):
    rank = first_ref.shape[0]
    first = lax.dot_general(
        power_ref[...], first_ref[...], LANES_BY_LANES, precision=HIGHEST, preferred_element_type=F32
    )
    gram = lax.dot_general(first, first, ROWS_BY_ROWS, precision=HIGHEST, preferred_element_type=F32)
    inverse_factor(gram, work_ref, second_ref)
    both = jnp.dot(second_ref[...], first_ref[...], precision=HIGHEST, preferred_element_type=F32)
    maps_ref[:rank, :] = both
    maps_ref[rank:, :] = lax.dot_general(both, both, ROWS_BY_ROWS, precision=HIGHEST, preferred_element_type=F32)


IN_VMEM = pl.BlockSpec(memory_space=pltpu.VMEM)


def first_pass(power):
    square = (power.shape[1],) * 2
    return pl.pallas_call(
        first_pass_kernel,
        out_shape=jax.ShapeDtypeStruct(square, F32),
        in_specs=[IN_VMEM],
        out_specs=IN_VMEM,
        scratch_shapes=[pltpu.VMEM(square, F32)],
        compiler_params=pltpu.CompilerParams(vmem_limit_bytes=VMEM_BYTES),
        cost_estimate=QR_COST,
    )(power)


def second_pass(power, first):
    square = first.shape
    return pl.pallas_call(
        second_pass_kernel,
        out_shape=jax.ShapeDtypeStruct((2 * square[0], square[1]), F32),
        in_specs=[IN_VMEM, IN_VMEM],
        out_specs=IN_VMEM,
        scratch_shapes=[pltpu.VMEM(square, F32)] * 2,
        compiler_params=pltpu.CompilerParams(vmem_limit_bytes=VMEM_BYTES),
        cost_estimate=QR_COST,
    )(power, first)


def factor_kernel(grads_ref, errors_ref, power_ref, terms_ref, sum_ref):
    rank = power_ref.shape[1]
    split = jnp.concatenate(pieces(power_ref[...], 2), axis=1)
    products = lax.dot_general(split, grads_ref[...], ROWS_BY_ROWS, preferred_element_type=F32)
    products += lax.dot_general(split, errors_ref[...], ROWS_BY_ROWS, preferred_element_type=F32)

    @pl.when(pl.program_id(0) == 0)
    def _():
        sum_ref[...] = products

    @pl.when(pl.program_id(0) > 0)
    def _():
        sum_ref[...] += products

    terms_ref[...] = sum_ref[:rank, :] + sum_ref[rank:, :]


def factor_terms(grads, errors, power):
    rows, cols = grads.shape
    rank = power.shape[1]
    tiled = pl.BlockSpec((TILE, cols), lambda i: (i, 0))
    return pl.pallas_call(
        factor_kernel,
        grid=(rows // TILE,),
        out_shape=jax.ShapeDtypeStruct((rank, cols), F32),
        in_specs=[tiled, tiled, pl.BlockSpec((TILE, rank), lambda i: (i, 0))],
        out_specs=whole((rank, cols)),
        scratch_shapes=[pltpu.VMEM((2 * rank, cols), F32)],
        compiler_params=pltpu.CompilerParams(vmem_limit_bytes=VMEM_BYTES),
    )(grads, errors, power)


def output_kernel(replicas, own_ref, grads_ref, errors_ref, power_ref, share_ref, maps_ref, terms_ref,
                  avg_ref, new_ref, q_ref, split_ref):
    def decompressed(rows):
        high, low = pieces(rows, 2)
        return jnp.dot(jnp.concatenate([high, high, low], axis=1), split_ref[...], preferred_element_type=F32)

    @pl.when(pl.program_id(0) == 0)
    def _():
        mapped = jnp.dot(maps_ref[...], terms_ref[...], precision=HIGHEST, preferred_element_type=F32)
        mapped = mapped * (1.0 / replicas)
        rank = power_ref.shape[1]
        q_ref[...] = mapped[:rank, :].T
        high, low = pieces(mapped[rank:, :], 2)
        split_ref[...] = jnp.concatenate([high, low, high], axis=0)
        avg_ref[...] = decompressed(share_ref[...]).astype(BF16)

    merged = grads_ref[...].astype(F32) + errors_ref[...].astype(F32)
    new_ref[...] = (merged - decompressed(power_ref[...])).astype(BF16)


def outputs(grads, errors, power, maps, terms, replicas, own):
    rows, cols = grads.shape
    rank = power.shape[1]
    share = rows // replicas
    tiled = pl.BlockSpec((TILE, cols), lambda i, own: (i, 0))
    return pl.pallas_call(
        functools.partial(output_kernel, replicas),
        grid_spec=pltpu.PrefetchScalarGridSpec(
            num_scalar_prefetch=1,
            grid=(rows // TILE,),
            in_specs=[
                tiled,
                tiled,
                pl.BlockSpec((TILE, rank), lambda i, own: (i, 0)),
                pl.BlockSpec((share, rank), lambda i, own: (own[0], 0)),
                whole((2 * rank, rank)),
                whole((rank, cols)),
            ],
            out_specs=(whole((share, cols)), tiled, whole((cols, rank))),
            scratch_shapes=[pltpu.VMEM((3 * rank, cols), BF16)],
        ),
        out_shape=(
            jax.ShapeDtypeStruct((share, cols), BF16),
            jax.ShapeDtypeStruct((rows, cols), BF16),
            jax.ShapeDtypeStruct((cols, rank), F32),
        ),
        compiler_params=pltpu.CompilerParams(vmem_limit_bytes=OUTPUT_VMEM_BYTES),
    )(own, grads, errors, power, power, maps, terms)


def scatter_sum(values, axes):
    count = lax.axis_size(axes)
    shares = lax.all_to_all(values, axes, 0, 0, tiled=True)
    return shares.reshape(count, values.shape[0] // count, values.shape[1]).sum(axis=0)


def gather(values, axes):
    count = lax.axis_size(axes)
    copies = jnp.broadcast_to(values[None], (count, *values.shape)).reshape(-1, values.shape[1])
    return lax.all_to_all(copies, axes, 0, 0, tiled=True)


def exchange_sum(values, axes):
    return gather(values, axes).reshape(lax.axis_size(axes), *values.shape).sum(axis=0)


def body(grads, errors, q_init):
    replicas = lax.axis_size(DP)
    power = power_terms(grads, errors, q_init)
    power = scatter_sum(power, "core")
    power = scatter_sum(power, ("y", "x"))
    power = exchange_sum(power, "near")
    power = exchange_sum(power, "far")
    power = gather(power, ("y", "x"))
    power = gather(power, "core")

    terms = factor_terms(grads, errors, power)
    first = first_pass(power)
    terms = scatter_sum(terms, ("near", "y"))
    terms, first = lax.optimization_barrier((terms, first))
    maps = second_pass(power, first)
    terms = exchange_sum(terms, "far")
    terms, maps = lax.optimization_barrier((terms, maps))
    terms = gather(terms, ("near", "y"))
    own = lax.axis_index(DP).reshape(1)
    return outputs(grads, errors, power, maps, terms, replicas, own)


def solution(mesh):
    near = 4
    fine = Mesh(mesh.devices.reshape(4, near, 4, 4, 2), ("far", "near", "y", "x", "core"))
    placed = (P(DP, TENSOR), P(DP, TENSOR), P(TENSOR, None))
    return jax.shard_map(
        body,
        mesh=fine,
        in_specs=placed,
        out_specs=(P(DP, TENSOR), P(DP, TENSOR), P(TENSOR, None)),
        check_vma=False,
    )
```

```python
import functools

import jax
import jax.numpy as jnp
from jax import lax
from jax.experimental import pallas as pl
from jax.experimental.pallas import tpu as pltpu
from jax.sharding import Mesh, PartitionSpec as P

F32 = jnp.float32
BF16 = jnp.bfloat16
HIGHEST = lax.Precision.HIGHEST
ROWS_BY_ROWS = (((0,), (0,)), ((), ()))
LANES_BY_LANES = (((1,), (1,)), ((), ()))
WIDTH = 8
TILE = 512
CHUNK = 256
VMEM_BYTES = 16 << 20
QR_COST = pl.CostEstimate(flops=7_000_000_000, bytes_accessed=1 << 20, transcendentals=0)

DP = ("far", "near", "y")
TENSOR = ("x", "core")
PLANE = ("y", "x", "core")


def pieces(values, count):
    parts = []
    for _ in range(count):
        part = values.astype(BF16)
        parts.append(part)
        values = values - part.astype(F32)
    return parts


def whole(ref_shape):
    return pl.BlockSpec(ref_shape, lambda *_: (0,) * len(ref_shape))


def load(sources, buffers, sems):
    chunks = sources[0].shape[0] // CHUNK

    def copy(k, n):
        rows = pl.ds(k * CHUNK, CHUNK)
        return pltpu.make_async_copy(sources[n].at[rows], buffers[n].at[rows], sems.at[k, n])

    for k in range(chunks):
        for n in range(len(sources)):
            copy(k, n).start()

    def wait(k):
        for n in range(len(sources)):
            copy(k, n).wait()

    return wait


def power_kernel(grads_ref, errors_ref, q_ref, power_ref, held_g, held_e, held_q, split_ref, q_sem, sems):
    cols, rank = q_ref.shape
    q_copy = pltpu.make_async_copy(q_ref, held_q, q_sem)
    q_copy.start()
    wait = load((grads_ref, errors_ref), (held_g, held_e), sems)
    q_copy.wait()
    for k, part in enumerate(pieces(held_q[...], 3)):
        split_ref[:cols, k * rank : (k + 1) * rank] = part
        split_ref[cols:, k * rank : (k + 1) * rank] = part
    for k in range(grads_ref.shape[0] // CHUNK):
        wait(k)
        rows = slice(k * CHUNK, (k + 1) * CHUNK)
        both = jnp.concatenate([held_g[rows, :], held_e[rows, :]], axis=1)
        products = jnp.dot(both, split_ref[...], preferred_element_type=F32)
        power_ref[rows, :] = products[:, :rank] + (products[:, rank : 2 * rank] + products[:, 2 * rank :])


IN_VMEM = pl.BlockSpec(memory_space=pltpu.VMEM)
IN_HBM = pl.BlockSpec(memory_space=pltpu.HBM)


def in_hbm(values):
    return pltpu.with_memory_space_constraint(values, pltpu.HBM)


def power_terms(grads, errors, q_init):
    rows, cols = grads.shape
    rank = q_init.shape[1]
    return pl.pallas_call(
        power_kernel,
        out_shape=jax.ShapeDtypeStruct((rows, rank), F32),
        in_specs=[IN_HBM] * 3,
        out_specs=IN_VMEM,
        scratch_shapes=[
            pltpu.VMEM((rows, cols), BF16),
            pltpu.VMEM((rows, cols), BF16),
            pltpu.VMEM((cols, rank), F32),
            pltpu.VMEM((2 * cols, 3 * rank), BF16),
            pltpu.SemaphoreType.DMA,
            pltpu.SemaphoreType.DMA((rows // CHUNK, 2)),
        ],
        compiler_params=pltpu.CompilerParams(vmem_limit_bytes=52 << 20),
    )(in_hbm(grads), in_hbm(errors), in_hbm(q_init))


def inverse_factor(gram, work_ref, inverse_ref):
    rank = gram.shape[0]
    lanes = lax.broadcasted_iota(jnp.int32, (WIDTH, rank), 1)
    subs = lax.broadcasted_iota(jnp.int32, (WIDTH, rank), 0)
    spread = lambda row: jnp.broadcast_to(row, (WIDTH, rank))
    work_ref[...] = gram
    for low in range(0, rank, WIDTH):
        own = work_ref[low : low + WIDTH, :]
        inside = (lanes >= low) & (lanes < low + WIDTH)
        columns = [spread(own[:, low + k : low + k + 1]) for k in range(WIDTH)]
        block = jnp.where(inside, (lanes - low == subs).astype(F32), own)
        forward = jnp.zeros((WIDTH, rank), F32)
        pivots = jnp.ones((WIDTH, rank), F32)
        reciprocals = jnp.zeros((WIDTH, rank), F32)
        for j in range(WIDTH):
            heads = [spread(column[j : j + 1, :]) for column in columns[j:]]
            row = spread(block[j : j + 1, :])
            forward = jnp.where(subs == j, row, forward)
            pivots = jnp.where(subs == j, heads[0], pivots)
            reciprocal = 1.0 / heads[0]
            reciprocals = jnp.where(subs == j, reciprocal, reciprocals)
            factor = jnp.where(subs == j, 0.0, columns[j] * reciprocal)
            for k in range(j + 1, WIDTH):
                columns[k] = columns[k] - factor * heads[k - j]
            block = block - factor * row
        inverse_ref[low : low + WIDTH, :] = jnp.where(lanes < low + WIDTH, forward * lax.rsqrt(pivots), 0.0)
        block = block * reciprocals
        solved = [spread(block[k : k + 1, :]) for k in range(WIDTH)]
        for at in range(low + WIDTH, rank, WIDTH):
            rest = work_ref[at : at + WIDTH, :]
            terms = [spread(rest[:, low + k : low + k + 1]) * solved[k] for k in range(WIDTH)]
            while len(terms) > 1:
                terms = [a + b for a, b in zip(terms[::2], terms[1::2], strict=True)]
            work_ref[at : at + WIDTH, :] = jnp.where(inside, 0.0, rest) - terms[0]


def first_pass_kernel(power_ref, first_ref, work_ref):
    power = power_ref[...]
    gram = lax.dot_general(power, power, ROWS_BY_ROWS, precision=HIGHEST, preferred_element_type=F32)
    inverse_factor(gram, work_ref, first_ref)


def second_pass_kernel(power_ref, first_ref, maps_ref, work_ref, second_ref):
    rank = first_ref.shape[0]
    first = lax.dot_general(
        power_ref[...], first_ref[...], LANES_BY_LANES, precision=HIGHEST, preferred_element_type=F32
    )
    gram = lax.dot_general(first, first, ROWS_BY_ROWS, precision=HIGHEST, preferred_element_type=F32)
    inverse_factor(gram, work_ref, second_ref)
    both = jnp.dot(second_ref[...], first_ref[...], precision=HIGHEST, preferred_element_type=F32)
    maps_ref[:rank, :] = both
    maps_ref[rank:, :] = lax.dot_general(both, both, ROWS_BY_ROWS, precision=HIGHEST, preferred_element_type=F32)


def first_pass(power):
    square = (power.shape[1],) * 2
    return pl.pallas_call(
        first_pass_kernel,
        out_shape=jax.ShapeDtypeStruct(square, F32),
        in_specs=[IN_VMEM],
        out_specs=IN_VMEM,
        scratch_shapes=[pltpu.VMEM(square, F32)],
        compiler_params=pltpu.CompilerParams(vmem_limit_bytes=32 << 20),
        cost_estimate=QR_COST,
    )(power)


def second_pass(power, first):
    square = first.shape
    return pl.pallas_call(
        second_pass_kernel,
        out_shape=jax.ShapeDtypeStruct((2 * square[0], square[1]), F32),
        in_specs=[IN_VMEM, IN_VMEM],
        out_specs=IN_VMEM,
        scratch_shapes=[pltpu.VMEM(square, F32)] * 2,
        compiler_params=pltpu.CompilerParams(vmem_limit_bytes=32 << 20),
        cost_estimate=QR_COST,
    )(power, first)


def factor_kernel(grads_ref, errors_ref, power_ref, terms_ref, sum_ref):
    rank = power_ref.shape[1]
    cols = grads_ref.shape[1]
    split = jnp.concatenate(pieces(power_ref[...], 2), axis=1)
    both = jnp.concatenate([grads_ref[...], errors_ref[...]], axis=1)
    products = lax.dot_general(split, both, ROWS_BY_ROWS, preferred_element_type=F32)
    products = products[:, :cols] + products[:, cols:]

    @pl.when(pl.program_id(0) == 0)
    def _():
        sum_ref[...] = products

    @pl.when(pl.program_id(0) > 0)
    def _():
        sum_ref[...] += products

    terms_ref[...] = sum_ref[:rank, :] + sum_ref[rank:, :]


def factor_terms(grads, errors, power):
    rows, cols = grads.shape
    rank = power.shape[1]
    tiled = pl.BlockSpec((TILE, cols), lambda i: (i, 0))
    return pl.pallas_call(
        factor_kernel,
        grid=(rows // TILE,),
        out_shape=jax.ShapeDtypeStruct((rank, cols), F32),
        in_specs=[tiled, tiled, pl.BlockSpec((TILE, rank), lambda i: (i, 0))],
        out_specs=whole((rank, cols)),
        scratch_shapes=[pltpu.VMEM((2 * rank, cols), F32)],
        compiler_params=pltpu.CompilerParams(vmem_limit_bytes=32 << 20),
    )(grads, errors, power)


def output_kernel(replicas, own_ref, grads_ref, errors_ref, power_ref, maps_ref, terms_ref, avg_ref, new_ref, q_ref,
                  held_g, held_e, held_new, split_ref, sems, out_sems):
    rank = power_ref.shape[1]
    share = avg_ref.shape[0]
    wait = load((grads_ref, errors_ref), (held_g, held_e), sems)

    def decompressed(rows):
        high, low = pieces(rows, 2)
        return jnp.dot(jnp.concatenate([high, high, low], axis=1), split_ref[...], preferred_element_type=F32)

    mapped = jnp.dot(maps_ref[...], terms_ref[...], precision=HIGHEST, preferred_element_type=F32)
    mapped = mapped * (1.0 / replicas)
    high, low = pieces(mapped[rank:, :], 2)
    split_ref[...] = jnp.concatenate([high, low, high], axis=0)
    writes = []
    for k in range(grads_ref.shape[0] // CHUNK):
        wait(k)
        rows = slice(k * CHUNK, (k + 1) * CHUNK)
        merged = held_g[rows, :].astype(F32) + held_e[rows, :].astype(F32)
        held_new[rows, :] = (merged - decompressed(power_ref[rows, :])).astype(BF16)
        chunk = pl.ds(k * CHUNK, CHUNK)
        writes.append(pltpu.make_async_copy(held_new.at[chunk], new_ref.at[chunk], out_sems.at[k]))
        writes[-1].start()
    own = power_ref[pl.ds(pl.multiple_of(own_ref[0] * share, share), share), :]
    avg_ref[...] = decompressed(own).astype(BF16)
    q_ref[...] = mapped[:rank, :].T
    for write in writes:
        write.wait()


def outputs(grads, errors, power, maps, terms, replicas, own):
    rows, cols = grads.shape
    rank = power.shape[1]
    chunks = rows // CHUNK
    return pl.pallas_call(
        functools.partial(output_kernel, replicas),
        in_specs=[pl.BlockSpec(memory_space=pltpu.SMEM), IN_HBM, IN_HBM, IN_VMEM, IN_VMEM, IN_VMEM],
        out_specs=(IN_VMEM, IN_HBM, IN_VMEM),
        out_shape=(
            jax.ShapeDtypeStruct((rows // replicas, cols), BF16),
            jax.ShapeDtypeStruct((rows, cols), BF16),
            jax.ShapeDtypeStruct((cols, rank), F32),
        ),
        scratch_shapes=[
            pltpu.VMEM((rows, cols), BF16),
            pltpu.VMEM((rows, cols), BF16),
            pltpu.VMEM((rows, cols), BF16),
            pltpu.VMEM((3 * rank, cols), BF16),
            pltpu.SemaphoreType.DMA((chunks, 2)),
            pltpu.SemaphoreType.DMA((chunks,)),
        ],
        compiler_params=pltpu.CompilerParams(vmem_limit_bytes=52 << 20),
    )(own, in_hbm(grads), in_hbm(errors), power, maps, terms)


def scatter_sum(values, axes):
    count = lax.axis_size(axes)
    shares = lax.all_to_all(values, axes, 0, 0, tiled=True)
    return shares.reshape(count, values.shape[0] // count, values.shape[1]).sum(axis=0)


def gather(values, axes):
    count = lax.axis_size(axes)
    copies = jnp.broadcast_to(values[None], (count, *values.shape)).reshape(-1, values.shape[1])
    return lax.all_to_all(copies, axes, 0, 0, tiled=True)


def exchange_sum(values, axes):
    return gather(values, axes).reshape(lax.axis_size(axes), *values.shape).sum(axis=0)


def body(grads, errors, q_init):
    replicas = lax.axis_size(DP)
    power = power_terms(grads, errors, q_init)
    power = scatter_sum(power, PLANE)
    power = exchange_sum(power, "near")
    power = exchange_sum(power, "far")
    power = gather(power, PLANE)

    terms = factor_terms(grads, errors, power)
    first = first_pass(power)
    terms = scatter_sum(terms, ("near", "y"))
    terms, first = lax.optimization_barrier((terms, first))
    maps = second_pass(power, first)
    terms = exchange_sum(terms, "far")
    own = lax.axis_index(DP).reshape(1)
    terms, maps, own = lax.optimization_barrier((terms, maps, own))
    terms = gather(terms, ("near", "y"))
    return outputs(grads, errors, power, maps, terms, replicas, own)


def solution(mesh):
    near = 4
    fine = Mesh(mesh.devices.reshape(4, near, 4, 4, 2), ("far", "near", "y", "x", "core"))
    placed = (P(DP, TENSOR), P(DP, TENSOR), P(TENSOR, None))
    return jax.shard_map(
        body,
        mesh=fine,
        in_specs=placed,
        out_specs=(P(DP, TENSOR), P(DP, TENSOR), P(TENSOR, None)),
        check_vma=False,
    )
```

```python
import functools

import jax
import jax.numpy as jnp
from jax import lax
from jax.experimental import pallas as pl
from jax.experimental.pallas import tpu as pltpu
from jax.sharding import Mesh, PartitionSpec as P

F32 = jnp.float32
BF16 = jnp.bfloat16
HIGHEST = lax.Precision.HIGHEST
ROWS_BY_ROWS = (((0,), (0,)), ((), ()))
LANES_BY_LANES = (((1,), (1,)), ((), ()))
WIDTH = 8
CHUNK = 1024
VMEM_BYTES = 16 << 20
QR_COST = pl.CostEstimate(flops=7_000_000_000, bytes_accessed=1 << 20, transcendentals=0)

DP = ("far", "near", "y")
TENSOR = ("x", "core")


def pieces(values, count):
    parts = []
    for _ in range(count):
        part = values.astype(BF16)
        parts.append(part)
        values = values - part.astype(F32)
    return parts


def load(sources, buffers, sems):
    chunks = sources[0].shape[0] // CHUNK

    def copy(k, n):
        rows = pl.ds(k * CHUNK, CHUNK)
        return pltpu.make_async_copy(sources[n].at[rows], buffers[n].at[rows], sems.at[k, n])

    for k in range(chunks):
        for n in range(len(sources)):
            copy(k, n).start()

    def wait(k):
        for n in range(len(sources)):
            copy(k, n).wait()

    return wait


def power_kernel(grads_ref, errors_ref, q_ref, power_ref, held_g, held_e, held_q, split_ref, q_sem, sems):
    cols, rank = q_ref.shape
    q_copy = pltpu.make_async_copy(q_ref, held_q, q_sem)
    q_copy.start()
    wait = load((grads_ref, errors_ref), (held_g, held_e), sems)
    q_copy.wait()
    for k, part in enumerate(pieces(held_q[...], 3)):
        split_ref[:cols, k * rank : (k + 1) * rank] = part
        split_ref[cols:, k * rank : (k + 1) * rank] = part
    for k in range(grads_ref.shape[0] // CHUNK):
        wait(k)
        rows = slice(k * CHUNK, (k + 1) * CHUNK)
        both = jnp.concatenate([held_g[rows, :], held_e[rows, :]], axis=1)
        products = jnp.dot(both, split_ref[...], preferred_element_type=F32)
        power_ref[rows, :] = products[:, :rank] + (products[:, rank : 2 * rank] + products[:, 2 * rank :])


IN_VMEM = pl.BlockSpec(memory_space=pltpu.VMEM)
IN_HBM = pl.BlockSpec(memory_space=pltpu.HBM)


def in_hbm(values):
    return pltpu.with_memory_space_constraint(values, pltpu.HBM)


def power_terms(grads, errors, q_init):
    rows, cols = grads.shape
    rank = q_init.shape[1]
    return pl.pallas_call(
        power_kernel,
        out_shape=jax.ShapeDtypeStruct((rows, rank), F32),
        in_specs=[IN_HBM] * 3,
        out_specs=IN_VMEM,
        scratch_shapes=[
            pltpu.VMEM((rows, cols), BF16),
            pltpu.VMEM((rows, cols), BF16),
            pltpu.VMEM((cols, rank), F32),
            pltpu.VMEM((2 * cols, 3 * rank), BF16),
            pltpu.SemaphoreType.DMA,
            pltpu.SemaphoreType.DMA((rows // CHUNK, 2)),
        ],
        compiler_params=pltpu.CompilerParams(vmem_limit_bytes=52 << 20),
    )(in_hbm(grads), in_hbm(errors), in_hbm(q_init))


def inverse_factor(gram, work_ref, inverse_ref):
    rank = gram.shape[0]
    lanes = lax.broadcasted_iota(jnp.int32, (WIDTH, rank), 1)
    subs = lax.broadcasted_iota(jnp.int32, (WIDTH, rank), 0)
    spread = lambda row: jnp.broadcast_to(row, (WIDTH, rank))
    work_ref[...] = gram
    for low in range(0, rank, WIDTH):
        own = work_ref[low : low + WIDTH, :]
        inside = (lanes >= low) & (lanes < low + WIDTH)
        columns = [spread(own[:, low + k : low + k + 1]) for k in range(WIDTH)]
        block = jnp.where(inside, (lanes - low == subs).astype(F32), own)
        forward = jnp.zeros((WIDTH, rank), F32)
        pivots = jnp.ones((WIDTH, rank), F32)
        reciprocals = jnp.zeros((WIDTH, rank), F32)
        for j in range(WIDTH):
            heads = [spread(column[j : j + 1, :]) for column in columns[j:]]
            row = spread(block[j : j + 1, :])
            forward = jnp.where(subs == j, row, forward)
            pivots = jnp.where(subs == j, heads[0], pivots)
            reciprocal = 1.0 / heads[0]
            reciprocals = jnp.where(subs == j, reciprocal, reciprocals)
            factor = jnp.where(subs == j, 0.0, columns[j] * reciprocal)
            for k in range(j + 1, WIDTH):
                columns[k] = columns[k] - factor * heads[k - j]
            block = block - factor * row
        inverse_ref[low : low + WIDTH, :] = jnp.where(lanes < low + WIDTH, forward * lax.rsqrt(pivots), 0.0)
        block = block * reciprocals
        solved = [spread(block[k : k + 1, :]) for k in range(WIDTH)]
        for at in range(low + WIDTH, rank, WIDTH):
            rest = work_ref[at : at + WIDTH, :]
            terms = [spread(rest[:, low + k : low + k + 1]) * solved[k] for k in range(WIDTH)]
            while len(terms) > 1:
                terms = [a + b for a, b in zip(terms[::2], terms[1::2], strict=True)]
            work_ref[at : at + WIDTH, :] = jnp.where(inside, 0.0, rest) - terms[0]


def first_pass_kernel(power_ref, first_ref, work_ref):
    power = power_ref[...]
    gram = lax.dot_general(power, power, ROWS_BY_ROWS, precision=HIGHEST, preferred_element_type=F32)
    inverse_factor(gram, work_ref, first_ref)


def second_pass_kernel(power_ref, first_ref, maps_ref, work_ref, second_ref):
    rank = first_ref.shape[0]
    first = lax.dot_general(
        power_ref[...], first_ref[...], LANES_BY_LANES, precision=HIGHEST, preferred_element_type=F32
    )
    gram = lax.dot_general(first, first, ROWS_BY_ROWS, precision=HIGHEST, preferred_element_type=F32)
    inverse_factor(gram, work_ref, second_ref)
    both = jnp.dot(second_ref[...], first_ref[...], precision=HIGHEST, preferred_element_type=F32)
    maps_ref[:rank, :] = both
    maps_ref[rank:, :] = lax.dot_general(both, both, ROWS_BY_ROWS, precision=HIGHEST, preferred_element_type=F32)


def first_pass(power):
    square = (power.shape[1],) * 2
    return pl.pallas_call(
        first_pass_kernel,
        out_shape=jax.ShapeDtypeStruct(square, F32),
        in_specs=[IN_VMEM],
        out_specs=IN_VMEM,
        scratch_shapes=[pltpu.VMEM(square, F32)],
        compiler_params=pltpu.CompilerParams(vmem_limit_bytes=32 << 20),
        cost_estimate=QR_COST,
    )(power)


def second_pass(power, first):
    square = first.shape
    return pl.pallas_call(
        second_pass_kernel,
        out_shape=jax.ShapeDtypeStruct((2 * square[0], square[1]), F32),
        in_specs=[IN_VMEM, IN_VMEM],
        out_specs=IN_VMEM,
        scratch_shapes=[pltpu.VMEM(square, F32)] * 2,
        compiler_params=pltpu.CompilerParams(vmem_limit_bytes=32 << 20),
        cost_estimate=QR_COST,
    )(power, first)


def factor_kernel(grads_ref, errors_ref, power_ref, terms_ref):
    rank, cols = terms_ref.shape
    split = jnp.concatenate(pieces(power_ref[...], 2), axis=1)
    both = jnp.concatenate([grads_ref[...], errors_ref[...]], axis=1)
    products = lax.dot_general(split, both, ROWS_BY_ROWS, preferred_element_type=F32)
    products = products[:, :cols] + products[:, cols:]
    terms_ref[...] = products[:rank, :] + products[rank:, :]


def factor_terms(grads, errors, power):
    return pl.pallas_call(
        factor_kernel,
        out_shape=jax.ShapeDtypeStruct((power.shape[1], grads.shape[1]), F32),
        in_specs=[IN_VMEM] * 3,
        out_specs=IN_VMEM,
        compiler_params=pltpu.CompilerParams(vmem_limit_bytes=32 << 20),
    )(grads, errors, power)


def output_kernel(replicas, own_ref, grads_ref, errors_ref, power_ref, maps_ref, terms_ref, avg_ref, new_ref, q_ref,
                  held_g, held_e, held_new, held_avg, held_q, sems, out_sems, avg_sem, q_sem):
    rank = power_ref.shape[1]
    share = avg_ref.shape[0]
    wait = load((grads_ref, errors_ref), (held_g, held_e), sems)
    writes = []

    def write(held, out, sem):
        writes.append(pltpu.make_async_copy(held, out, sem))
        writes[-1].start()

    def left(values):
        high, low = pieces(values, 2)
        return jnp.concatenate([high, high, low], axis=1)

    def right(values):
        high, low = pieces(values, 2)
        return jnp.concatenate([high, low, high], axis=0)

    def product(values, stacked):
        return jnp.dot(left(values), stacked, preferred_element_type=F32)

    terms = right(terms_ref[...] * (1.0 / replicas))
    mapped = right(product(maps_ref[rank:, :], terms))
    for k in range(grads_ref.shape[0] // CHUNK):
        wait(k)
        rows = slice(k * CHUNK, (k + 1) * CHUNK)
        merged = held_g[rows, :].astype(F32) + held_e[rows, :].astype(F32)
        held_new[rows, :] = (merged - product(power_ref[rows, :], mapped)).astype(BF16)
        chunk = pl.ds(k * CHUNK, CHUNK)
        write(held_new.at[chunk], new_ref.at[chunk], out_sems.at[k])
        if k == 0:
            own = power_ref[pl.ds(pl.multiple_of(own_ref[0] * share, share), share), :]
            held_avg[...] = product(own, mapped).astype(BF16)
            write(held_avg, avg_ref, avg_sem)
            held_q[...] = product(maps_ref[:rank, :], terms).T
            write(held_q, q_ref, q_sem)
    for copy in writes:
        copy.wait()


def outputs(grads, errors, power, maps, terms, replicas, own):
    rows, cols = grads.shape
    rank = power.shape[1]
    share = rows // replicas
    chunks = rows // CHUNK
    return pl.pallas_call(
        functools.partial(output_kernel, replicas),
        in_specs=[pl.BlockSpec(memory_space=pltpu.SMEM), IN_HBM, IN_HBM, IN_VMEM, IN_VMEM, IN_VMEM],
        out_specs=(IN_HBM, IN_HBM, IN_HBM),
        out_shape=(
            jax.ShapeDtypeStruct((share, cols), BF16),
            jax.ShapeDtypeStruct((rows, cols), BF16),
            jax.ShapeDtypeStruct((cols, rank), F32),
        ),
        scratch_shapes=[
            pltpu.VMEM((rows, cols), BF16),
            pltpu.VMEM((rows, cols), BF16),
            pltpu.VMEM((rows, cols), BF16),
            pltpu.VMEM((share, cols), BF16),
            pltpu.VMEM((cols, rank), F32),
            pltpu.SemaphoreType.DMA((chunks, 2)),
            pltpu.SemaphoreType.DMA((chunks,)),
            pltpu.SemaphoreType.DMA,
            pltpu.SemaphoreType.DMA,
        ],
        compiler_params=pltpu.CompilerParams(vmem_limit_bytes=52 << 20),
    )(own, in_hbm(grads), in_hbm(errors), power, maps, terms)


def scatter_sum(values, axes):
    count = lax.axis_size(axes)
    shares = lax.all_to_all(values, axes, 0, 0, tiled=True)
    return shares.reshape(count, values.shape[0] // count, values.shape[1]).sum(axis=0)


def gather(values, axes):
    count = lax.axis_size(axes)
    copies = jnp.broadcast_to(values[None], (count, *values.shape)).reshape(-1, values.shape[1])
    return lax.all_to_all(copies, axes, 0, 0, tiled=True)


def exchange_sum(values, axes):
    return gather(values, axes).reshape(lax.axis_size(axes), *values.shape).sum(axis=0)


def body(grads, errors, q_init):
    replicas = lax.axis_size(DP)
    power = power_terms(grads, errors, q_init)
    power = scatter_sum(power, "core")
    power = scatter_sum(power, ("y", "x"))
    power = exchange_sum(power, "near")
    power = exchange_sum(power, "far")
    power = gather(power, ("y", "x"))
    power = gather(power, "core")

    terms = factor_terms(grads, errors, power)
    first = first_pass(power)
    own = lax.axis_index(DP).reshape(1)
    terms = scatter_sum(terms, ("near", "y"))
    terms, first, own = lax.optimization_barrier((terms, first, own))
    terms = exchange_sum(terms, "far")
    terms, first = lax.optimization_barrier((terms, first))
    maps = second_pass(power, first)
    terms = gather(terms, ("near", "y"))
    return outputs(grads, errors, power, maps, terms, replicas, own)


def solution(mesh):
    near = 4
    fine = Mesh(mesh.devices.reshape(4, near, 4, 4, 2), ("far", "near", "y", "x", "core"))
    placed = (P(DP, TENSOR), P(DP, TENSOR), P(TENSOR, None))
    return jax.shard_map(
        body,
        mesh=fine,
        in_specs=placed,
        out_specs=(P(DP, TENSOR), P(DP, TENSOR), P(TENSOR, None)),
        check_vma=False,
    )
```

```python
import functools

import jax
import jax.numpy as jnp
from jax import lax
from jax.experimental import pallas as pl
from jax.experimental.pallas import tpu as pltpu
from jax.sharding import Mesh, PartitionSpec as P

F32 = jnp.float32
BF16 = jnp.bfloat16
HIGHEST = lax.Precision.HIGHEST
ROWS_BY_ROWS = (((0,), (0,)), ((), ()))
LANES_BY_LANES = (((1,), (1,)), ((), ()))
WIDTH = 8
CHUNK = 1024
VMEM_BYTES = 16 << 20
QR_COST = pl.CostEstimate(flops=7_000_000_000, bytes_accessed=1 << 20, transcendentals=0)

NEAR = 4

DP = ("z", "y")
TENSOR = ("x", "core")


def pieces(values, count):
    parts = []
    for _ in range(count):
        part = values.astype(BF16)
        parts.append(part)
        values = values - part.astype(F32)
    return parts


def load(sources, buffers, sems):
    chunks = sources[0].shape[0] // CHUNK

    def copy(k, n):
        rows = pl.ds(k * CHUNK, CHUNK)
        return pltpu.make_async_copy(sources[n].at[rows], buffers[n].at[rows], sems.at[k, n])

    for k in range(chunks):
        for n in range(len(sources)):
            copy(k, n).start()

    def wait(k):
        for n in range(len(sources)):
            copy(k, n).wait()

    return wait


def power_kernel(grads_ref, errors_ref, q_ref, power_ref, held_g, held_e, held_q, split_ref, q_sem, sems):
    cols, rank = q_ref.shape
    q_copy = pltpu.make_async_copy(q_ref, held_q, q_sem)
    q_copy.start()
    wait = load((grads_ref, errors_ref), (held_g, held_e), sems)
    q_copy.wait()
    for k, part in enumerate(pieces(held_q[...], 3)):
        split_ref[:cols, k * rank : (k + 1) * rank] = part
        split_ref[cols:, k * rank : (k + 1) * rank] = part
    for k in range(grads_ref.shape[0] // CHUNK):
        wait(k)
        rows = slice(k * CHUNK, (k + 1) * CHUNK)
        both = jnp.concatenate([held_g[rows, :], held_e[rows, :]], axis=1)
        products = jnp.dot(both, split_ref[...], preferred_element_type=F32)
        power_ref[rows, :] = products[:, :rank] + (products[:, rank : 2 * rank] + products[:, 2 * rank :])


IN_VMEM = pl.BlockSpec(memory_space=pltpu.VMEM)
IN_HBM = pl.BlockSpec(memory_space=pltpu.HBM)


def in_hbm(values):
    return pltpu.with_memory_space_constraint(values, pltpu.HBM)


def power_terms(grads, errors, q_init):
    rows, cols = grads.shape
    rank = q_init.shape[1]
    return pl.pallas_call(
        power_kernel,
        out_shape=jax.ShapeDtypeStruct((rows, rank), F32),
        in_specs=[IN_HBM] * 3,
        out_specs=IN_VMEM,
        scratch_shapes=[
            pltpu.VMEM((rows, cols), BF16),
            pltpu.VMEM((rows, cols), BF16),
            pltpu.VMEM((cols, rank), F32),
            pltpu.VMEM((2 * cols, 3 * rank), BF16),
            pltpu.SemaphoreType.DMA,
            pltpu.SemaphoreType.DMA((rows // CHUNK, 2)),
        ],
        compiler_params=pltpu.CompilerParams(vmem_limit_bytes=52 << 20),
    )(in_hbm(grads), in_hbm(errors), in_hbm(q_init))


def inverse_factor(gram, work_ref, inverse_ref):
    rank = gram.shape[0]
    lanes = lax.broadcasted_iota(jnp.int32, (WIDTH, rank), 1)
    subs = lax.broadcasted_iota(jnp.int32, (WIDTH, rank), 0)
    spread = lambda row: jnp.broadcast_to(row, (WIDTH, rank))
    work_ref[...] = gram
    for low in range(0, rank, WIDTH):
        own = work_ref[low : low + WIDTH, :]
        inside = (lanes >= low) & (lanes < low + WIDTH)
        columns = [spread(own[:, low + k : low + k + 1]) for k in range(WIDTH)]
        block = jnp.where(inside, (lanes - low == subs).astype(F32), own)
        forward = jnp.zeros((WIDTH, rank), F32)
        pivots = jnp.ones((WIDTH, rank), F32)
        reciprocals = jnp.zeros((WIDTH, rank), F32)
        for j in range(WIDTH):
            heads = [spread(column[j : j + 1, :]) for column in columns[j:]]
            row = spread(block[j : j + 1, :])
            forward = jnp.where(subs == j, row, forward)
            pivots = jnp.where(subs == j, heads[0], pivots)
            reciprocal = 1.0 / heads[0]
            reciprocals = jnp.where(subs == j, reciprocal, reciprocals)
            factor = jnp.where(subs == j, 0.0, columns[j] * reciprocal)
            for k in range(j + 1, WIDTH):
                columns[k] = columns[k] - factor * heads[k - j]
            block = block - factor * row
        inverse_ref[low : low + WIDTH, :] = jnp.where(lanes < low + WIDTH, forward * lax.rsqrt(pivots), 0.0)
        block = block * reciprocals
        solved = [spread(block[k : k + 1, :]) for k in range(WIDTH)]
        for at in range(low + WIDTH, rank, WIDTH):
            rest = work_ref[at : at + WIDTH, :]
            terms = [spread(rest[:, low + k : low + k + 1]) * solved[k] for k in range(WIDTH)]
            while len(terms) > 1:
                terms = [a + b for a, b in zip(terms[::2], terms[1::2], strict=True)]
            work_ref[at : at + WIDTH, :] = jnp.where(inside, 0.0, rest) - terms[0]


def first_pass_kernel(power_ref, first_ref, gram_ref, work_ref):
    power = power_ref[...]
    gram = lax.dot_general(power, power, ROWS_BY_ROWS, precision=HIGHEST, preferred_element_type=F32)
    inverse_factor(gram, work_ref, first_ref)
    first = lax.dot_general(power, first_ref[...], LANES_BY_LANES, precision=HIGHEST, preferred_element_type=F32)
    gram_ref[...] = lax.dot_general(first, first, ROWS_BY_ROWS, precision=HIGHEST, preferred_element_type=F32)


def second_pass_kernel(first_ref, gram_ref, maps_ref, work_ref, second_ref):
    rank = first_ref.shape[0]
    inverse_factor(gram_ref[...], work_ref, second_ref)
    both = jnp.dot(second_ref[...], first_ref[...], precision=HIGHEST, preferred_element_type=F32)
    maps_ref[:rank, :] = both
    maps_ref[rank:, :] = lax.dot_general(both, both, ROWS_BY_ROWS, precision=HIGHEST, preferred_element_type=F32)


def first_pass(power):
    square = (power.shape[1],) * 2
    return pl.pallas_call(
        first_pass_kernel,
        out_shape=(jax.ShapeDtypeStruct(square, F32),) * 2,
        in_specs=[IN_VMEM],
        out_specs=(IN_VMEM, IN_VMEM),
        scratch_shapes=[pltpu.VMEM(square, F32)],
        compiler_params=pltpu.CompilerParams(vmem_limit_bytes=VMEM_BYTES),
        cost_estimate=QR_COST,
    )(power)


def second_pass(first, gram):
    rank = gram.shape[0]
    return pl.pallas_call(
        second_pass_kernel,
        out_shape=jax.ShapeDtypeStruct((2 * rank, rank), F32),
        in_specs=[IN_VMEM, IN_VMEM],
        out_specs=IN_VMEM,
        scratch_shapes=[pltpu.VMEM((rank, rank), F32)] * 2,
        compiler_params=pltpu.CompilerParams(vmem_limit_bytes=VMEM_BYTES),
        cost_estimate=QR_COST,
    )(first, gram)


def factor_kernel(grads_ref, errors_ref, power_ref, terms_ref):
    rank, cols = terms_ref.shape
    split = jnp.concatenate(pieces(power_ref[...], 2), axis=1)
    both = jnp.concatenate([grads_ref[...], errors_ref[...]], axis=1)
    products = lax.dot_general(split, both, ROWS_BY_ROWS, preferred_element_type=F32)
    products = products[:, :cols] + products[:, cols:]
    terms_ref[...] = products[:rank, :] + products[rank:, :]


def factor_terms(grads, errors, power):
    return pl.pallas_call(
        factor_kernel,
        out_shape=jax.ShapeDtypeStruct((power.shape[1], grads.shape[1]), F32),
        in_specs=[IN_VMEM] * 3,
        out_specs=IN_VMEM,
        compiler_params=pltpu.CompilerParams(vmem_limit_bytes=32 << 20),
    )(grads, errors, power)


def output_kernel(replicas, own_ref, grads_ref, errors_ref, power_ref, maps_ref, terms_ref, avg_ref, new_ref, q_ref,
                  held_g, held_e, held_new, held_avg, held_q, sems, out_sems, avg_sem, q_sem):
    rank = power_ref.shape[1]
    share = avg_ref.shape[0]
    wait = load((grads_ref, errors_ref), (held_g, held_e), sems)
    writes = []

    def write(held, out, sem):
        writes.append(pltpu.make_async_copy(held, out, sem))
        writes[-1].start()

    def left(values):
        high, low = pieces(values, 2)
        return jnp.concatenate([high, high, low], axis=1)

    def right(values):
        high, low = pieces(values, 2)
        return jnp.concatenate([high, low, high], axis=0)

    def product(values, stacked):
        return jnp.dot(left(values), stacked, preferred_element_type=F32)

    terms = right(terms_ref[...] * (1.0 / replicas))
    mapped = right(product(maps_ref[rank:, :], terms))
    for k in range(grads_ref.shape[0] // CHUNK):
        wait(k)
        rows = slice(k * CHUNK, (k + 1) * CHUNK)
        merged = held_g[rows, :].astype(F32) + held_e[rows, :].astype(F32)
        held_new[rows, :] = (merged - product(power_ref[rows, :], mapped)).astype(BF16)
        chunk = pl.ds(k * CHUNK, CHUNK)
        write(held_new.at[chunk], new_ref.at[chunk], out_sems.at[k])
        if k == 0:
            own = power_ref[pl.ds(pl.multiple_of(own_ref[0] * share, share), share), :]
            held_avg[...] = product(own, mapped).astype(BF16)
            write(held_avg, avg_ref, avg_sem)
            held_q[...] = product(maps_ref[:rank, :], terms).T
            write(held_q, q_ref, q_sem)
    for copy in writes:
        copy.wait()


def outputs(grads, errors, power, maps, terms, replicas, own):
    rows, cols = grads.shape
    rank = power.shape[1]
    share = rows // replicas
    chunks = rows // CHUNK
    return pl.pallas_call(
        functools.partial(output_kernel, replicas),
        in_specs=[pl.BlockSpec(memory_space=pltpu.SMEM), IN_HBM, IN_HBM, IN_VMEM, IN_VMEM, IN_VMEM],
        out_specs=(IN_HBM, IN_HBM, IN_HBM),
        out_shape=(
            jax.ShapeDtypeStruct((share, cols), BF16),
            jax.ShapeDtypeStruct((rows, cols), BF16),
            jax.ShapeDtypeStruct((cols, rank), F32),
        ),
        scratch_shapes=[
            pltpu.VMEM((rows, cols), BF16),
            pltpu.VMEM((rows, cols), BF16),
            pltpu.VMEM((rows, cols), BF16),
            pltpu.VMEM((share, cols), BF16),
            pltpu.VMEM((cols, rank), F32),
            pltpu.SemaphoreType.DMA((chunks, 2)),
            pltpu.SemaphoreType.DMA((chunks,)),
            pltpu.SemaphoreType.DMA,
            pltpu.SemaphoreType.DMA,
        ],
        compiler_params=pltpu.CompilerParams(vmem_limit_bytes=52 << 20),
    )(own, in_hbm(grads), in_hbm(errors), power, maps, terms)


def exchange(values, axes, groups):
    return lax.all_to_all(values, axes, 0, 0, axis_index_groups=groups, tiled=True)


def members(axes, groups):
    return lax.axis_size(axes) if groups is None else len(groups[0])


def scatter_sum(values, axes, groups=None):
    count = members(axes, groups)
    shares = exchange(values, axes, groups)
    return shares.reshape(count, values.shape[0] // count, values.shape[1]).sum(axis=0)


def gather(values, axes, groups=None):
    copies = jnp.broadcast_to(values[None], (members(axes, groups), *values.shape)).reshape(-1, values.shape[1])
    return exchange(copies, axes, groups)


def exchange_sum(values, axes, groups):
    return gather(values, axes, groups).reshape(members(axes, groups), *values.shape).sum(axis=0)


def z_groups(length, width):
    blocks = length // NEAR

    def device(block, share, y):
        turn = NEAR // 2 if 2 * block >= blocks else 0
        return (block * NEAR + (share + turn) % NEAR) * width + y

    shares = [(share, y) for share in range(NEAR) for y in range(width)]
    near = [[device(block, *share) for share in shares] for block in range(blocks)]
    far = [[device(block, *share) for block in range(blocks)] for share in shares]
    return near, far


def body(grads, errors, q_init):
    replicas = lax.axis_size(DP)
    power = power_terms(grads, errors, q_init)
    near, far = z_groups(lax.axis_size("z"), 1)
    power = scatter_sum(power, "core")
    power = scatter_sum(power, ("y", "x"))
    power = exchange_sum(power, "z", near)
    power = exchange_sum(power, "z", far)
    power = gather(power, ("y", "x"))
    power = gather(power, "core")

    near, far = z_groups(lax.axis_size("z"), lax.axis_size("y"))
    terms = factor_terms(grads, errors, power)
    first = first_pass(power)
    own = lax.axis_index(DP).reshape(1)
    terms = scatter_sum(terms, DP, near)
    terms, first, own = lax.optimization_barrier((terms, first, own))
    terms = exchange_sum(terms, DP, far)
    terms, first = lax.optimization_barrier((terms, first))
    maps = second_pass(*first)
    terms = gather(terms, DP, near)
    return outputs(grads, errors, power, maps, terms, replicas, own)


def solution(mesh):
    fine = Mesh(mesh.devices.reshape(16, 4, 4, 2), ("z", "y", "x", "core"))
    placed = (P(DP, TENSOR), P(DP, TENSOR), P(TENSOR, None))
    return jax.shard_map(
        body,
        mesh=fine,
        in_specs=placed,
        out_specs=(P(DP, TENSOR), P(DP, TENSOR), P(TENSOR, None)),
        check_vma=False,
    )
```

```python
import functools

import jax
import jax.numpy as jnp
from jax import lax
from jax.experimental import pallas as pl
from jax.experimental.pallas import tpu as pltpu
from jax.sharding import Mesh, PartitionSpec as P

F32 = jnp.float32
BF16 = jnp.bfloat16
HIGHEST = lax.Precision.HIGHEST
ROWS_BY_ROWS = (((0,), (0,)), ((), ()))
LANES_BY_LANES = (((1,), (1,)), ((), ()))
WIDTH = 8
CHUNK = 512
VMEM_BYTES = 16 << 20
QR_COST = pl.CostEstimate(flops=7_000_000_000, bytes_accessed=1 << 20, transcendentals=0)

NEAR = 4
HALF_COST = pl.CostEstimate(flops=1_200_000_000, bytes_accessed=2 << 20, transcendentals=0)

DP = ("z", "y")
TENSOR = ("x", "core")


def pieces(values, count):
    parts = []
    for _ in range(count):
        part = values.astype(BF16)
        parts.append(part)
        values = values - part.astype(F32)
    return parts


def load(sources, buffers, sems, starts, size):
    def copy(k, n):
        rows = pl.ds(pl.multiple_of(starts[k], size), size)
        return pltpu.make_async_copy(sources[n].at[rows], buffers[n].at[pl.ds(k * size, size)], sems.at[k, n])

    for k in range(len(starts)):
        for n in range(len(sources)):
            copy(k, n).start()

    def wait(k):
        for n in range(len(sources)):
            copy(k, n).wait()

    return wait


def power_kernel(half_ref, grads_ref, errors_ref, q_ref, power_ref, held_g, held_e, held_q, split_ref, q_sem, sems):
    cols, rank = q_ref.shape
    rows = power_ref.shape[0]
    q_copy = pltpu.make_async_copy(q_ref, held_q, q_sem)
    q_copy.start()
    starts = [half_ref[0] * rows + k * CHUNK for k in range(rows // CHUNK)]
    wait = load((grads_ref, errors_ref), (held_g, held_e), sems, starts, CHUNK)
    q_copy.wait()
    for k, part in enumerate(pieces(held_q[...], 3)):
        split_ref[:cols, k * rank : (k + 1) * rank] = part
        split_ref[cols:, k * rank : (k + 1) * rank] = part
    for k in range(len(starts)):
        wait(k)
        chunk = slice(k * CHUNK, (k + 1) * CHUNK)
        both = jnp.concatenate([held_g[chunk, :], held_e[chunk, :]], axis=1)
        products = jnp.dot(both, split_ref[...], preferred_element_type=F32)
        power_ref[chunk, :] = products[:, :rank] + (products[:, rank : 2 * rank] + products[:, 2 * rank :])


IN_SMEM = pl.BlockSpec(memory_space=pltpu.SMEM)
IN_VMEM = pl.BlockSpec(memory_space=pltpu.VMEM)
IN_HBM = pl.BlockSpec(memory_space=pltpu.HBM)


def in_hbm(values):
    return pltpu.with_memory_space_constraint(values, pltpu.HBM)


def power_terms(grads, errors, q_init, half, keep):
    rows, cols = grads.shape[0] // 2, grads.shape[1]
    rank = q_init.shape[1]
    power = jax.ShapeDtypeStruct((rows, rank), F32)
    held = jax.ShapeDtypeStruct((rows, cols), BF16)
    return pl.pallas_call(
        power_kernel,
        out_shape=(power, held) if keep else power,
        in_specs=[IN_SMEM, IN_HBM, IN_HBM, IN_HBM],
        out_specs=(IN_VMEM,) * 2 if keep else IN_VMEM,
        scratch_shapes=[pltpu.VMEM((rows, cols), BF16)] * (1 if keep else 2)
        + [
            pltpu.VMEM((cols, rank), F32),
            pltpu.VMEM((2 * cols, 3 * rank), BF16),
            pltpu.SemaphoreType.DMA,
            pltpu.SemaphoreType.DMA((rows // CHUNK, 2)),
        ],
        compiler_params=pltpu.CompilerParams(vmem_limit_bytes=52 << 20),
        cost_estimate=HALF_COST,
    )(half, in_hbm(grads), in_hbm(errors), in_hbm(q_init))


def inverse_factor(gram, work_ref, inverse_ref):
    rank = gram.shape[0]
    lanes = lax.broadcasted_iota(jnp.int32, (WIDTH, rank), 1)
    subs = lax.broadcasted_iota(jnp.int32, (WIDTH, rank), 0)
    spread = lambda row: jnp.broadcast_to(row, (WIDTH, rank))
    work_ref[...] = gram
    for low in range(0, rank, WIDTH):
        own = work_ref[low : low + WIDTH, :]
        inside = (lanes >= low) & (lanes < low + WIDTH)
        columns = [spread(own[:, low + k : low + k + 1]) for k in range(WIDTH)]
        block = jnp.where(inside, (lanes - low == subs).astype(F32), own)
        forward = jnp.zeros((WIDTH, rank), F32)
        pivots = jnp.ones((WIDTH, rank), F32)
        reciprocals = jnp.zeros((WIDTH, rank), F32)
        for j in range(WIDTH):
            heads = [spread(column[j : j + 1, :]) for column in columns[j:]]
            row = spread(block[j : j + 1, :])
            forward = jnp.where(subs == j, row, forward)
            pivots = jnp.where(subs == j, heads[0], pivots)
            reciprocal = 1.0 / heads[0]
            reciprocals = jnp.where(subs == j, reciprocal, reciprocals)
            factor = jnp.where(subs == j, 0.0, columns[j] * reciprocal)
            for k in range(j + 1, WIDTH):
                columns[k] = columns[k] - factor * heads[k - j]
            block = block - factor * row
        inverse_ref[low : low + WIDTH, :] = jnp.where(lanes < low + WIDTH, forward * lax.rsqrt(pivots), 0.0)
        block = block * reciprocals
        solved = [spread(block[k : k + 1, :]) for k in range(WIDTH)]
        for at in range(low + WIDTH, rank, WIDTH):
            rest = work_ref[at : at + WIDTH, :]
            terms = [spread(rest[:, low + k : low + k + 1]) * solved[k] for k in range(WIDTH)]
            while len(terms) > 1:
                terms = [a + b for a, b in zip(terms[::2], terms[1::2], strict=True)]
            work_ref[at : at + WIDTH, :] = jnp.where(inside, 0.0, rest) - terms[0]


def gram_of(halves):
    terms = [
        lax.dot_general(half, half, ROWS_BY_ROWS, precision=HIGHEST, preferred_element_type=F32) for half in halves
    ]
    return terms[0] + terms[1]


def first_pass_kernel(kept_ref, other_ref, first_ref, work_ref):
    inverse_factor(gram_of([kept_ref[...], other_ref[...]]), work_ref, first_ref)


def second_pass_kernel(kept_ref, other_ref, first_ref, maps_ref, work_ref, second_ref):
    rank = first_ref.shape[0]
    first = [
        lax.dot_general(half[...], first_ref[...], LANES_BY_LANES, precision=HIGHEST, preferred_element_type=F32)
        for half in (kept_ref, other_ref)
    ]
    inverse_factor(gram_of(first), work_ref, second_ref)
    both = jnp.dot(second_ref[...], first_ref[...], precision=HIGHEST, preferred_element_type=F32)
    maps_ref[:rank, :] = both
    maps_ref[rank:, :] = lax.dot_general(both, both, ROWS_BY_ROWS, precision=HIGHEST, preferred_element_type=F32)


def first_pass(power):
    square = (power[0].shape[1],) * 2
    return pl.pallas_call(
        first_pass_kernel,
        out_shape=jax.ShapeDtypeStruct(square, F32),
        in_specs=[IN_VMEM, IN_VMEM],
        out_specs=IN_VMEM,
        scratch_shapes=[pltpu.VMEM(square, F32)],
        compiler_params=pltpu.CompilerParams(vmem_limit_bytes=32 << 20),
        cost_estimate=QR_COST,
    )(*power)


def second_pass(power, first):
    square = first.shape
    return pl.pallas_call(
        second_pass_kernel,
        out_shape=jax.ShapeDtypeStruct((2 * square[0], square[1]), F32),
        in_specs=[IN_VMEM] * 3,
        out_specs=IN_VMEM,
        scratch_shapes=[pltpu.VMEM(square, F32)] * 2,
        compiler_params=pltpu.CompilerParams(vmem_limit_bytes=32 << 20),
        cost_estimate=QR_COST,
    )(*power, first)


def power_by_merged(power, grads, errors):
    rank, cols = power.shape[1], grads.shape[1]
    split = jnp.concatenate(pieces(power, 2), axis=1)
    both = jnp.concatenate([grads, errors], axis=1)
    products = lax.dot_general(split, both, ROWS_BY_ROWS, preferred_element_type=F32)
    products = products[:, :cols] + products[:, cols:]
    return products[:rank, :] + products[rank:, :]


def kept_factor_kernel(half_ref, grads_ref, errors_ref, power_ref, terms_ref, other_ref, held_g, held_e, sems, other_sem):
    count = power_ref.shape[0]
    wait = load((grads_ref, errors_ref), (held_g, held_e), sems, [half_ref[0] * count], count)
    rows = pl.ds(pl.multiple_of((1 - half_ref[0]) * count, count), count)
    other = pltpu.make_async_copy(errors_ref.at[rows], other_ref, other_sem)
    other.start()
    wait(0)
    terms_ref[...] = power_by_merged(power_ref[...], held_g[...], held_e[...])
    other.wait()


def other_factor_kernel(grads_ref, errors_ref, power_ref, before_ref, terms_ref):
    terms_ref[...] = before_ref[...] + power_by_merged(power_ref[...], grads_ref[...], errors_ref[...])


def kept_factor_terms(grads, errors, power, half):
    rows, rank = power.shape
    cols = grads.shape[1]
    return pl.pallas_call(
        kept_factor_kernel,
        out_shape=(jax.ShapeDtypeStruct((rank, cols), F32), jax.ShapeDtypeStruct((rows, cols), BF16)),
        in_specs=[IN_SMEM, IN_HBM, IN_HBM, IN_VMEM],
        out_specs=(IN_VMEM, IN_VMEM),
        scratch_shapes=[pltpu.VMEM((rows, cols), BF16)] * 2 + [pltpu.SemaphoreType.DMA((1, 2)), pltpu.SemaphoreType.DMA],
        compiler_params=pltpu.CompilerParams(vmem_limit_bytes=32 << 20),
        cost_estimate=HALF_COST,
    )(half, in_hbm(grads), in_hbm(errors), power)


def other_factor_terms(grads, errors, power, before):
    return pl.pallas_call(
        other_factor_kernel,
        out_shape=jax.ShapeDtypeStruct(before.shape, F32),
        in_specs=[IN_VMEM] * 4,
        out_specs=IN_VMEM,
        compiler_params=pltpu.CompilerParams(vmem_limit_bytes=32 << 20),
        cost_estimate=HALF_COST,
    )(grads, errors, power, before)


def output_kernel(replicas, place_ref, grads_ref, errors_ref, kept_ref, other_ref, maps_ref, terms_ref,
                  avg_ref, new_ref, q_ref, held_g, held_e, held_new, held_avg, held_q, sems, out_sems, avg_sem, q_sem):
    rank = kept_ref.shape[1]
    count = kept_ref.shape[0]
    share = avg_ref.shape[0]
    kept_half, own = place_ref[0], place_ref[1]
    starts = [kept_half * count, (1 - kept_half) * count]
    wait = load((grads_ref, errors_ref), (held_g, held_e), sems, starts, count)
    writes = []

    def write(held, out, sem):
        writes.append(pltpu.make_async_copy(held, out, sem))
        writes[-1].start()

    def left(values):
        high, low = pieces(values, 2)
        return jnp.concatenate([high, high, low], axis=1)

    def right(values):
        high, low = pieces(values, 2)
        return jnp.concatenate([high, low, high], axis=0)

    def product(values, stacked):
        return jnp.dot(left(values), stacked, preferred_element_type=F32)

    terms = right(terms_ref[...] * (1.0 / replicas))
    mapped = right(product(maps_ref[rank:, :], terms))
    for k, power_ref in enumerate((kept_ref, other_ref)):
        wait(k)
        rows = slice(k * count, (k + 1) * count)
        merged = held_g[rows, :].astype(F32) + held_e[rows, :].astype(F32)
        held_new[rows, :] = (merged - product(power_ref[...], mapped)).astype(BF16)
        out = pl.ds(pl.multiple_of(starts[k], count), count)
        write(held_new.at[pl.ds(k * count, count)], new_ref.at[out], out_sems.at[k])
        if k == 0:
            per_half = count // share
            rows = pl.ds(pl.multiple_of(lax.rem(own, per_half) * share, share), share)
            here = jnp.broadcast_to(own // per_half == kept_half, (share, rank))
            held_avg[...] = product(jnp.where(here, kept_ref[rows, :], other_ref[rows, :]), mapped).astype(BF16)
            write(held_avg, avg_ref, avg_sem)
            held_q[...] = product(maps_ref[:rank, :], terms).T
            write(held_q, q_ref, q_sem)
    for copy in writes:
        copy.wait()


def outputs(grads, errors, power, maps, terms, replicas, place):
    rows, cols = grads.shape
    rank = power[0].shape[1]
    share = rows // replicas
    return pl.pallas_call(
        functools.partial(output_kernel, replicas),
        in_specs=[IN_SMEM, IN_HBM, IN_HBM] + [IN_VMEM] * 4,
        out_specs=(IN_HBM, IN_HBM, IN_HBM),
        out_shape=(
            jax.ShapeDtypeStruct((share, cols), BF16),
            jax.ShapeDtypeStruct((rows, cols), BF16),
            jax.ShapeDtypeStruct((cols, rank), F32),
        ),
        scratch_shapes=[
            pltpu.VMEM((rows, cols), BF16),
            pltpu.VMEM((rows, cols), BF16),
            pltpu.VMEM((rows, cols), BF16),
            pltpu.VMEM((share, cols), BF16),
            pltpu.VMEM((cols, rank), F32),
            pltpu.SemaphoreType.DMA((2, 2)),
            pltpu.SemaphoreType.DMA((2,)),
            pltpu.SemaphoreType.DMA,
            pltpu.SemaphoreType.DMA,
        ],
        compiler_params=pltpu.CompilerParams(vmem_limit_bytes=52 << 20),
    )(place, in_hbm(grads), in_hbm(errors), *power, maps, terms)


def exchange(values, axes, groups):
    return lax.all_to_all(values, axes, 0, 0, axis_index_groups=groups, tiled=True)


def members(axes, groups):
    return lax.axis_size(axes) if groups is None else len(groups[0])


def scatter_sum(values, axes, groups=None):
    count = members(axes, groups)
    shares = exchange(values, axes, groups)
    return shares.reshape(count, values.shape[0] // count, values.shape[1]).sum(axis=0)


def gather(values, axes, groups=None):
    copies = jnp.broadcast_to(values[None], (members(axes, groups), *values.shape)).reshape(-1, values.shape[1])
    return exchange(copies, axes, groups)


def exchange_sum(values, axes, groups):
    return gather(values, axes, groups).reshape(members(axes, groups), *values.shape).sum(axis=0)


def z_groups(length, width):
    blocks = length // NEAR

    def device(block, share, y):
        turn = NEAR // 2 if 2 * block >= blocks else 0
        return (block * NEAR + (share + turn) % NEAR) * width + y

    shares = [(share, y) for share in range(NEAR) for y in range(width)]
    near = [[device(block, *share) for share in shares] for block in range(blocks)]
    far = [[device(block, *share) for block in range(blocks)] for share in shares]
    return near, far


def swap(values):
    return lax.ppermute(values, "core", [(0, 1), (1, 0)])


def body(grads, errors, q_init):
    replicas = lax.axis_size(DP)
    half = lax.axis_index("core").reshape(1)
    sent, other_grads = power_terms(grads, errors, q_init, 1 - half, keep=True)
    received = swap(sent)
    power = power_terms(grads, errors, q_init, half, keep=False) + received

    near, far = z_groups(lax.axis_size("z"), 1)
    power = scatter_sum(power, ("y", "x"))
    power = exchange_sum(power, "z", near)
    power = exchange_sum(power, "z", far)
    power = gather(power, ("y", "x"))
    power = (power, swap(power))

    near, far = z_groups(lax.axis_size("z"), lax.axis_size("y"))
    terms, other_errors = kept_factor_terms(grads, errors, power[0], half)
    terms = other_factor_terms(other_grads, other_errors, power[1], terms)
    first = first_pass(power)
    place = jnp.concatenate([half, lax.axis_index(DP).reshape(1)])
    terms = scatter_sum(terms, DP, near)
    terms, first, place = lax.optimization_barrier((terms, first, place))
    terms = exchange_sum(terms, DP, far)
    terms, first = lax.optimization_barrier((terms, first))
    maps = second_pass(power, first)
    terms = gather(terms, DP, near)
    return outputs(grads, errors, power, maps, terms, replicas, place)


def solution(mesh):
    fine = Mesh(mesh.devices.reshape(16, 4, 4, 2), ("z", "y", "x", "core"))
    placed = (P(DP, TENSOR), P(DP, TENSOR), P(TENSOR, None))
    return jax.shard_map(
        body,
        mesh=fine,
        in_specs=placed,
        out_specs=(P(DP, TENSOR), P(DP, TENSOR), P(TENSOR, None)),
        check_vma=False,
    )
```

```python
import functools

import jax
import jax.numpy as jnp
from jax import lax
from jax.experimental import pallas as pl
from jax.experimental.pallas import tpu as pltpu
from jax.sharding import Mesh, PartitionSpec as P

F32 = jnp.float32
BF16 = jnp.bfloat16
HIGHEST = lax.Precision.HIGHEST
ROWS_BY_ROWS = (((0,), (0,)), ((), ()))
LANES_BY_LANES = (((1,), (1,)), ((), ()))
WIDTH = 16
CHUNK = 512
VMEM_BYTES = 16 << 20
QR_COST = pl.CostEstimate(flops=7_000_000_000, bytes_accessed=1 << 20, transcendentals=0)

NEAR = 4
HALF_COST = pl.CostEstimate(flops=1_200_000_000, bytes_accessed=2 << 20, transcendentals=0)

DP = ("z", "y")
TENSOR = ("x", "core")


def pieces(values, count):
    parts = []
    for _ in range(count):
        part = values.astype(BF16)
        parts.append(part)
        values = values - part.astype(F32)
    return parts


def half_rows(half, count):
    return pl.ds(pl.multiple_of(half * count, count), count)


def load(sources, buffers, sems, starts, size):
    def copy(k, n):
        rows = pl.ds(pl.multiple_of(starts[k], size), size)
        return pltpu.make_async_copy(sources[n].at[rows], buffers[n].at[pl.ds(k * size, size)], sems.at[k, n])

    for k in range(len(starts)):
        for n in range(len(sources)):
            copy(k, n).start()

    def wait(k):
        for n in range(len(sources)):
            copy(k, n).wait()

    return wait


def power_product(grads, errors, split):
    rank = split.shape[1] // 3
    products = jnp.dot(jnp.concatenate([grads, errors], axis=1), split, preferred_element_type=F32)
    return products[:, :rank] + (products[:, rank : 2 * rank] + products[:, 2 * rank :])


def split_q(q, split_ref):
    cols, rank = q.shape
    for k, part in enumerate(pieces(q, 3)):
        split_ref[:cols, k * rank : (k + 1) * rank] = part
        split_ref[cols:, k * rank : (k + 1) * rank] = part


def sent_power_kernel(half_ref, grads_ref, errors_ref, q_ref, power_ref, own_g,
                      other_g, other_e, held_q, split_ref, q_sem, sems, own_sem):
    rows = power_ref.shape[0]
    q_copy = pltpu.make_async_copy(q_ref, held_q, q_sem)
    q_copy.start()
    starts = [(1 - half_ref[0]) * rows + k * CHUNK for k in range(rows // CHUNK)]
    wait = load((grads_ref, errors_ref), (other_g, other_e), sems, starts, CHUNK)
    own = pltpu.make_async_copy(grads_ref.at[half_rows(half_ref[0], rows)], own_g, own_sem)
    own.start()
    q_copy.wait()
    split_q(held_q[...], split_ref)
    for k in range(len(starts)):
        wait(k)
        chunk = slice(k * CHUNK, (k + 1) * CHUNK)
        power_ref[chunk, :] = power_product(other_g[chunk, :], other_e[chunk, :], split_ref[...])
    own.wait()


def kept_power_kernel(half_ref, grads_ref, errors_ref, q_ref, power_ref, own_e, split_ref, sem):
    own = pltpu.make_async_copy(errors_ref.at[half_rows(half_ref[0], power_ref.shape[0])], own_e, sem)
    own.start()
    split_q(q_ref[...], split_ref)
    own.wait()
    power_ref[...] = power_product(grads_ref[...], own_e[...], split_ref[...])


IN_SMEM = pl.BlockSpec(memory_space=pltpu.SMEM)
IN_VMEM = pl.BlockSpec(memory_space=pltpu.VMEM)
IN_HBM = pl.BlockSpec(memory_space=pltpu.HBM)


def in_hbm(values):
    return pltpu.with_memory_space_constraint(values, pltpu.HBM)


def sent_power_terms(grads, errors, q_init, half):
    rows, cols = grads.shape[0] // 2, grads.shape[1]
    rank = q_init.shape[1]
    held = jax.ShapeDtypeStruct((rows, cols), BF16)
    return pl.pallas_call(
        sent_power_kernel,
        out_shape=(jax.ShapeDtypeStruct((rows, rank), F32), held),
        in_specs=[IN_SMEM, IN_HBM, IN_HBM, IN_HBM],
        out_specs=(IN_VMEM,) * 2,
        scratch_shapes=[
            pltpu.VMEM((rows, cols), BF16),
            pltpu.VMEM((rows, cols), BF16),
            pltpu.VMEM((cols, rank), F32),
            pltpu.VMEM((2 * cols, 3 * rank), BF16),
            pltpu.SemaphoreType.DMA,
            pltpu.SemaphoreType.DMA((rows // CHUNK, 2)),
            pltpu.SemaphoreType.DMA,
        ],
        compiler_params=pltpu.CompilerParams(vmem_limit_bytes=52 << 20),
        cost_estimate=HALF_COST,
    )(half, in_hbm(grads), in_hbm(errors), in_hbm(q_init))


def kept_power_terms(own_grads, errors, q_init, half):
    cols, rank = q_init.shape
    rows = own_grads.shape[0]
    return pl.pallas_call(
        kept_power_kernel,
        out_shape=jax.ShapeDtypeStruct((rows, rank), F32),
        in_specs=[IN_SMEM, IN_VMEM, IN_HBM, IN_VMEM],
        out_specs=IN_VMEM,
        scratch_shapes=[
            pltpu.VMEM((rows, cols), BF16),
            pltpu.VMEM((2 * cols, 3 * rank), BF16),
            pltpu.SemaphoreType.DMA,
        ],
        compiler_params=pltpu.CompilerParams(vmem_limit_bytes=32 << 20),
        cost_estimate=HALF_COST,
    )(half, own_grads, in_hbm(errors), q_init)


def inverse_factor(gram, work_ref, inverse_ref):
    rank = gram.shape[0]
    lanes = lax.broadcasted_iota(jnp.int32, (WIDTH, rank), 1)
    subs = lax.broadcasted_iota(jnp.int32, (WIDTH, rank), 0)
    spread = lambda row: jnp.broadcast_to(row, (WIDTH, rank))
    work_ref[...] = gram
    for low in range(0, rank, WIDTH):
        own = work_ref[low : low + WIDTH, :]
        inside = (lanes >= low) & (lanes < low + WIDTH)
        columns = [spread(own[:, low + k : low + k + 1]) for k in range(WIDTH)]
        block = jnp.where(inside, (lanes - low == subs).astype(F32), own)
        forward = jnp.zeros((WIDTH, rank), F32)
        pivots = jnp.ones((WIDTH, rank), F32)
        reciprocals = jnp.zeros((WIDTH, rank), F32)
        for j in range(WIDTH):
            heads = [spread(column[j : j + 1, :]) for column in columns[j:]]
            row = spread(block[j : j + 1, :])
            forward = jnp.where(subs == j, row, forward)
            pivots = jnp.where(subs == j, heads[0], pivots)
            reciprocal = 1.0 / heads[0]
            reciprocals = jnp.where(subs == j, reciprocal, reciprocals)
            factor = jnp.where(subs == j, 0.0, columns[j] * reciprocal)
            for k in range(j + 1, WIDTH):
                columns[k] = columns[k] - factor * heads[k - j]
            block = block - factor * row
        inverse_ref[low : low + WIDTH, :] = jnp.where(lanes < low + WIDTH, forward * lax.rsqrt(pivots), 0.0)
        block = block * reciprocals
        solved = [spread(block[k : k + 1, :]) for k in range(WIDTH)]
        for at in range(low + WIDTH, rank, WIDTH):
            rest = work_ref[at : at + WIDTH, :]
            terms = [spread(rest[:, low + k : low + k + 1]) * solved[k] for k in range(WIDTH)]
            while len(terms) > 1:
                terms = [a + b for a, b in zip(terms[::2], terms[1::2], strict=True)]
            work_ref[at : at + WIDTH, :] = jnp.where(inside, 0.0, rest) - terms[0]


def gram_of(halves):
    terms = [
        lax.dot_general(half, half, ROWS_BY_ROWS, precision=HIGHEST, preferred_element_type=F32) for half in halves
    ]
    return terms[0] + terms[1]


def first_pass_kernel(kept_ref, other_ref, first_ref, work_ref):
    inverse_factor(gram_of([kept_ref[...], other_ref[...]]), work_ref, first_ref)


def second_pass_kernel(kept_ref, other_ref, first_ref, grads_ref, maps_ref, held_ref, work_ref, second_ref, sem):
    rank = first_ref.shape[0]
    held = pltpu.make_async_copy(grads_ref, held_ref, sem)
    held.start()
    first = [
        lax.dot_general(half[...], first_ref[...], LANES_BY_LANES, precision=HIGHEST, preferred_element_type=F32)
        for half in (kept_ref, other_ref)
    ]
    inverse_factor(gram_of(first), work_ref, second_ref)
    both = jnp.dot(second_ref[...], first_ref[...], precision=HIGHEST, preferred_element_type=F32)
    maps_ref[:rank, :] = both
    maps_ref[rank:, :] = lax.dot_general(both, both, ROWS_BY_ROWS, precision=HIGHEST, preferred_element_type=F32)
    held.wait()


def first_pass(power):
    square = (power[0].shape[1],) * 2
    return pl.pallas_call(
        first_pass_kernel,
        out_shape=jax.ShapeDtypeStruct(square, F32),
        in_specs=[IN_VMEM, IN_VMEM],
        out_specs=IN_VMEM,
        scratch_shapes=[pltpu.VMEM(square, F32)],
        compiler_params=pltpu.CompilerParams(vmem_limit_bytes=32 << 20),
        cost_estimate=QR_COST,
    )(*power)


def second_pass(power, first, grads):
    square = first.shape
    return pl.pallas_call(
        second_pass_kernel,
        out_shape=(
            jax.ShapeDtypeStruct((2 * square[0], square[1]), F32),
            jax.ShapeDtypeStruct(grads.shape, grads.dtype),
        ),
        in_specs=[IN_VMEM] * 3 + [IN_HBM],
        out_specs=(IN_VMEM, IN_VMEM),
        scratch_shapes=[pltpu.VMEM(square, F32)] * 2 + [pltpu.SemaphoreType.DMA],
        compiler_params=pltpu.CompilerParams(vmem_limit_bytes=32 << 20),
        cost_estimate=QR_COST,
    )(*power, first, in_hbm(grads))


def power_by_merged(power, grads, errors):
    rank, cols = power.shape[1], grads.shape[1]
    split = jnp.concatenate(pieces(power, 2), axis=1)
    both = jnp.concatenate([grads, errors], axis=1)
    products = lax.dot_general(split, both, ROWS_BY_ROWS, preferred_element_type=F32)
    products = products[:, :cols] + products[:, cols:]
    return products[:rank, :] + products[rank:, :]


def kept_factor_kernel(half_ref, grads_ref, errors_ref, power_ref, terms_ref, other_ref, own_e, sem, other_sem):
    count = power_ref.shape[0]
    rows = half_rows(half_ref[0], count)
    own = pltpu.make_async_copy(errors_ref.at[rows], own_e, sem)
    other = pltpu.make_async_copy(errors_ref.at[half_rows(1 - half_ref[0], count)], other_ref, other_sem)
    own.start()
    other.start()
    own.wait()
    terms_ref[...] = power_by_merged(power_ref[...], grads_ref[rows, :], own_e[...])
    other.wait()


def other_factor_kernel(half_ref, grads_ref, errors_ref, power_ref, before_ref, terms_ref):
    rows = half_rows(1 - half_ref[0], power_ref.shape[0])
    terms_ref[...] = before_ref[...] + power_by_merged(power_ref[...], grads_ref[rows, :], errors_ref[...])


def kept_factor_terms(grads, errors, power, half):
    rows, rank = power.shape
    cols = grads.shape[1]
    return pl.pallas_call(
        kept_factor_kernel,
        out_shape=(jax.ShapeDtypeStruct((rank, cols), F32), jax.ShapeDtypeStruct((rows, cols), BF16)),
        in_specs=[IN_SMEM, IN_VMEM, IN_HBM, IN_VMEM],
        out_specs=(IN_VMEM, IN_VMEM),
        scratch_shapes=[pltpu.VMEM((rows, cols), BF16), pltpu.SemaphoreType.DMA, pltpu.SemaphoreType.DMA],
        compiler_params=pltpu.CompilerParams(vmem_limit_bytes=32 << 20),
        cost_estimate=HALF_COST,
    )(half, grads, in_hbm(errors), power)


def other_factor_terms(grads, other_errors, power, before, half):
    return pl.pallas_call(
        other_factor_kernel,
        out_shape=jax.ShapeDtypeStruct(before.shape, F32),
        in_specs=[IN_SMEM] + [IN_VMEM] * 4,
        out_specs=IN_VMEM,
        compiler_params=pltpu.CompilerParams(vmem_limit_bytes=32 << 20),
        cost_estimate=HALF_COST,
    )(half, grads, other_errors, power, before)


def output_kernel(replicas, place_ref, grads_ref, errors_ref, kept_ref, other_ref, maps_ref, terms_ref,
                  avg_ref, new_ref, q_ref, held_e, held_new, held_avg, held_q, sems, out_sems, avg_sem, q_sem):
    rank = kept_ref.shape[1]
    count = kept_ref.shape[0]
    share = avg_ref.shape[0]
    kept_half, own = place_ref[0], place_ref[1]
    starts = [kept_half * count, (1 - kept_half) * count]
    wait = load((errors_ref,), (held_e,), sems, starts, count)
    writes = []

    def write(held, out, sem):
        writes.append(pltpu.make_async_copy(held, out, sem))
        writes[-1].start()

    def left(values):
        high, low = pieces(values, 2)
        return jnp.concatenate([high, high, low], axis=1)

    def right(values):
        high, low = pieces(values, 2)
        return jnp.concatenate([high, low, high], axis=0)

    def product(values, stacked):
        return jnp.dot(left(values), stacked, preferred_element_type=F32)

    terms = right(terms_ref[...] * (1.0 / replicas))
    mapped = right(product(maps_ref[rank:, :], terms))
    for k, power_ref in enumerate((kept_ref, other_ref)):
        wait(k)
        rows = slice(k * count, (k + 1) * count)
        merged = grads_ref[pl.ds(pl.multiple_of(starts[k], count), count), :].astype(F32) + held_e[rows, :].astype(F32)
        held_new[rows, :] = (merged - product(power_ref[...], mapped)).astype(BF16)
        out = pl.ds(pl.multiple_of(starts[k], count), count)
        write(held_new.at[pl.ds(k * count, count)], new_ref.at[out], out_sems.at[k])
        if k == 0:
            per_half = count // share
            rows = pl.ds(pl.multiple_of(lax.rem(own, per_half) * share, share), share)
            here = jnp.broadcast_to(own // per_half == kept_half, (share, rank))
            held_avg[...] = product(jnp.where(here, kept_ref[rows, :], other_ref[rows, :]), mapped).astype(BF16)
            write(held_avg, avg_ref, avg_sem)
            held_q[...] = product(maps_ref[:rank, :], terms).T
            write(held_q, q_ref, q_sem)
    for copy in writes:
        copy.wait()


def outputs(grads, errors, power, maps, terms, replicas, place):
    rows, cols = grads.shape
    rank = power[0].shape[1]
    share = rows // replicas
    return pl.pallas_call(
        functools.partial(output_kernel, replicas),
        in_specs=[IN_SMEM, IN_VMEM, IN_HBM] + [IN_VMEM] * 4,
        out_specs=(IN_HBM, IN_HBM, IN_HBM),
        out_shape=(
            jax.ShapeDtypeStruct((share, cols), BF16),
            jax.ShapeDtypeStruct((rows, cols), BF16),
            jax.ShapeDtypeStruct((cols, rank), F32),
        ),
        scratch_shapes=[
            pltpu.VMEM((rows, cols), BF16),
            pltpu.VMEM((rows, cols), BF16),
            pltpu.VMEM((share, cols), BF16),
            pltpu.VMEM((cols, rank), F32),
            pltpu.SemaphoreType.DMA((2, 1)),
            pltpu.SemaphoreType.DMA((2,)),
            pltpu.SemaphoreType.DMA,
            pltpu.SemaphoreType.DMA,
        ],
        compiler_params=pltpu.CompilerParams(vmem_limit_bytes=16 << 20),
    )(place, grads, in_hbm(errors), *power, maps, terms)


def exchange(values, axes, groups):
    return lax.all_to_all(values, axes, 0, 0, axis_index_groups=groups, tiled=True)


def members(axes, groups):
    return lax.axis_size(axes) if groups is None else len(groups[0])


def scatter_sum(values, axes, groups=None):
    count = members(axes, groups)
    shares = exchange(values, axes, groups)
    return shares.reshape(count, values.shape[0] // count, values.shape[1]).sum(axis=0)


def gather(values, axes, groups=None):
    copies = jnp.broadcast_to(values[None], (members(axes, groups), *values.shape)).reshape(-1, values.shape[1])
    return exchange(copies, axes, groups)


def exchange_sum(values, axes, groups):
    return gather(values, axes, groups).reshape(members(axes, groups), *values.shape).sum(axis=0)


def z_groups(length, width):
    blocks = length // NEAR

    def device(block, share, y):
        turn = NEAR // 2 if 2 * block >= blocks else 0
        return (block * NEAR + (share + turn) % NEAR) * width + y

    shares = [(share, y) for share in range(NEAR) for y in range(width)]
    near = [[device(block, *share) for share in shares] for block in range(blocks)]
    far = [[device(block, *share) for block in range(blocks)] for share in shares]
    return near, far


def swap(values):
    return lax.ppermute(values, "core", [(0, 1), (1, 0)])


def body(grads, errors, q_init):
    replicas = lax.axis_size(DP)
    half = lax.axis_index("core").reshape(1)
    sent, own_grads = sent_power_terms(grads, errors, q_init, half)
    received = swap(sent)
    power = kept_power_terms(own_grads, errors, q_init, half) + received

    near, far = z_groups(lax.axis_size("z"), 1)
    power = scatter_sum(power, ("y", "x"))
    power = exchange_sum(power, "z", near)
    power = exchange_sum(power, "z", far)
    power = gather(power, ("y", "x"))
    power = (power, swap(power))

    near, far = z_groups(lax.axis_size("z"), lax.axis_size("y"))
    terms, other_errors = kept_factor_terms(grads, errors, power[0], half)
    terms = other_factor_terms(grads, other_errors, power[1], terms, half)
    first = first_pass(power)
    place = jnp.concatenate([half, lax.axis_index(DP).reshape(1)])
    terms = scatter_sum(terms, DP, near)
    terms, first, place = lax.optimization_barrier((terms, first, place))
    terms = exchange_sum(terms, DP, far)
    terms, first = lax.optimization_barrier((terms, first))
    maps, held_grads = second_pass(power, first, grads)
    terms = gather(terms, DP, near)
    return outputs(held_grads, errors, power, maps, terms, replicas, place)


def solution(mesh):
    fine = Mesh(mesh.devices.reshape(16, 4, 4, 2), ("z", "y", "x", "core"))
    placed = (P(DP, TENSOR), P(DP, TENSOR), P(TENSOR, None))
    return jax.shard_map(
        body,
        mesh=fine,
        in_specs=placed,
        out_specs=(P(DP, TENSOR), P(DP, TENSOR), P(TENSOR, None)),
        check_vma=False,
    )
```

```python
import functools

import jax
import jax.numpy as jnp
from jax import lax
from jax.experimental import pallas as pl
from jax.experimental.pallas import tpu as pltpu
from jax.sharding import Mesh, PartitionSpec as P

F32 = jnp.float32
BF16 = jnp.bfloat16
HIGHEST = lax.Precision.HIGHEST
ROWS_BY_ROWS = (((0,), (0,)), ((), ()))
LANES_BY_LANES = (((1,), (1,)), ((), ()))
WIDTH = 16
CHUNK = 512
PIECES = 2
VMEM_BYTES = 16 << 20
QR_COST = pl.CostEstimate(flops=7_000_000_000, bytes_accessed=1 << 20, transcendentals=0)

NEAR = 4
HALF_COST = pl.CostEstimate(flops=1_200_000_000, bytes_accessed=2 << 20, transcendentals=0)

DP = ("z", "y")
TENSOR = ("x", "core")


def pieces(values, count):
    parts = []
    for _ in range(count):
        part = values.astype(BF16)
        parts.append(part)
        values = values - part.astype(F32)
    return parts


def half_rows(half, count):
    return pl.ds(pl.multiple_of(half * count, count), count)


def load(sources, buffers, sems, starts, size):
    def copy(k, n):
        rows = pl.ds(pl.multiple_of(starts[k], size), size)
        return pltpu.make_async_copy(sources[n].at[rows], buffers[n].at[pl.ds(k * size, size)], sems.at[k, n])

    for k in range(len(starts)):
        for n in range(len(sources)):
            copy(k, n).start()

    def wait(k):
        for n in range(len(sources)):
            copy(k, n).wait()

    return wait


def power_product(grads, errors, split):
    rank = split.shape[1] // 3
    products = jnp.dot(jnp.concatenate([grads, errors], axis=1), split, preferred_element_type=F32)
    return products[:, :rank] + (products[:, rank : 2 * rank] + products[:, 2 * rank :])


def split_q(q, split_ref):
    cols, rank = q.shape
    for k, part in enumerate(pieces(q, 3)):
        split_ref[:cols, k * rank : (k + 1) * rank] = part
        split_ref[cols:, k * rank : (k + 1) * rank] = part


def sent_power_kernel(half_ref, grads_ref, errors_ref, q_ref, power_ref, own_g,
                      other_g, other_e, held_q, split_ref, q_sem, sems, own_sem):
    rows = power_ref.shape[0]
    q_copy = pltpu.make_async_copy(q_ref, held_q, q_sem)
    q_copy.start()
    starts = [(1 - half_ref[0]) * rows + k * CHUNK for k in range(rows // CHUNK)]
    wait = load((grads_ref, errors_ref), (other_g, other_e), sems, starts, CHUNK)
    own = pltpu.make_async_copy(grads_ref.at[half_rows(half_ref[0], rows)], own_g, own_sem)
    own.start()
    q_copy.wait()
    split_q(held_q[...], split_ref)
    for k in range(len(starts)):
        wait(k)
        chunk = slice(k * CHUNK, (k + 1) * CHUNK)
        power_ref[chunk, :] = power_product(other_g[chunk, :], other_e[chunk, :], split_ref[...])
    own.wait()


def kept_power_kernel(half_ref, grads_ref, errors_ref, q_ref, power_ref, own_e, split_ref, sem):
    own = pltpu.make_async_copy(errors_ref.at[half_rows(half_ref[0], power_ref.shape[0])], own_e, sem)
    own.start()
    split_q(q_ref[...], split_ref)
    own.wait()
    power_ref[...] = power_product(grads_ref[...], own_e[...], split_ref[...])


IN_SMEM = pl.BlockSpec(memory_space=pltpu.SMEM)
IN_VMEM = pl.BlockSpec(memory_space=pltpu.VMEM)
IN_HBM = pl.BlockSpec(memory_space=pltpu.HBM)


def in_hbm(values):
    return pltpu.with_memory_space_constraint(values, pltpu.HBM)


def sent_power_terms(grads, errors, q_init, half):
    rows, cols = grads.shape[0] // 2, grads.shape[1]
    rank = q_init.shape[1]
    held = jax.ShapeDtypeStruct((rows, cols), BF16)
    return pl.pallas_call(
        sent_power_kernel,
        out_shape=(jax.ShapeDtypeStruct((rows, rank), F32), held),
        in_specs=[IN_SMEM, IN_HBM, IN_HBM, IN_HBM],
        out_specs=(IN_VMEM,) * 2,
        scratch_shapes=[
            pltpu.VMEM((rows, cols), BF16),
            pltpu.VMEM((rows, cols), BF16),
            pltpu.VMEM((cols, rank), F32),
            pltpu.VMEM((2 * cols, 3 * rank), BF16),
            pltpu.SemaphoreType.DMA,
            pltpu.SemaphoreType.DMA((rows // CHUNK, 2)),
            pltpu.SemaphoreType.DMA,
        ],
        compiler_params=pltpu.CompilerParams(vmem_limit_bytes=52 << 20),
        cost_estimate=HALF_COST,
    )(half, in_hbm(grads), in_hbm(errors), in_hbm(q_init))


def kept_power_terms(own_grads, errors, q_init, half):
    cols, rank = q_init.shape
    rows = own_grads.shape[0]
    return pl.pallas_call(
        kept_power_kernel,
        out_shape=jax.ShapeDtypeStruct((rows, rank), F32),
        in_specs=[IN_SMEM, IN_VMEM, IN_HBM, IN_VMEM],
        out_specs=IN_VMEM,
        scratch_shapes=[
            pltpu.VMEM((rows, cols), BF16),
            pltpu.VMEM((2 * cols, 3 * rank), BF16),
            pltpu.SemaphoreType.DMA,
        ],
        compiler_params=pltpu.CompilerParams(vmem_limit_bytes=32 << 20),
        cost_estimate=HALF_COST,
    )(half, own_grads, in_hbm(errors), q_init)


def inverse_factor(gram, work_ref, inverse_ref):
    rank = gram.shape[0]
    lanes = lax.broadcasted_iota(jnp.int32, (WIDTH, rank), 1)
    subs = lax.broadcasted_iota(jnp.int32, (WIDTH, rank), 0)
    spread = lambda row: jnp.broadcast_to(row, (WIDTH, rank))
    work_ref[...] = gram
    for low in range(0, rank, WIDTH):
        own = work_ref[low : low + WIDTH, :]
        inside = (lanes >= low) & (lanes < low + WIDTH)
        columns = [spread(own[:, low + k : low + k + 1]) for k in range(WIDTH)]
        block = jnp.where(inside, (lanes - low == subs).astype(F32), own)
        forward = jnp.zeros((WIDTH, rank), F32)
        pivots = jnp.ones((WIDTH, rank), F32)
        reciprocals = jnp.zeros((WIDTH, rank), F32)
        for j in range(WIDTH):
            heads = [spread(column[j : j + 1, :]) for column in columns[j:]]
            row = spread(block[j : j + 1, :])
            forward = jnp.where(subs == j, row, forward)
            pivots = jnp.where(subs == j, heads[0], pivots)
            reciprocal = 1.0 / heads[0]
            reciprocals = jnp.where(subs == j, reciprocal, reciprocals)
            factor = jnp.where(subs == j, 0.0, columns[j] * reciprocal)
            for k in range(j + 1, WIDTH):
                columns[k] = columns[k] - factor * heads[k - j]
            block = block - factor * row
        inverse_ref[low : low + WIDTH, :] = jnp.where(lanes < low + WIDTH, forward * lax.rsqrt(pivots), 0.0)
        block = block * reciprocals
        solved = [spread(block[k : k + 1, :]) for k in range(WIDTH)]
        for at in range(low + WIDTH, rank, WIDTH):
            rest = work_ref[at : at + WIDTH, :]
            terms = [spread(rest[:, low + k : low + k + 1]) * solved[k] for k in range(WIDTH)]
            while len(terms) > 1:
                terms = [a + b for a, b in zip(terms[::2], terms[1::2], strict=True)]
            work_ref[at : at + WIDTH, :] = jnp.where(inside, 0.0, rest) - terms[0]


def gram_of(halves):
    terms = [
        lax.dot_general(half, half, ROWS_BY_ROWS, precision=HIGHEST, preferred_element_type=F32) for half in halves
    ]
    return terms[0] + terms[1]


def first_pass_kernel(kept_ref, other_ref, first_ref, work_ref):
    inverse_factor(gram_of([kept_ref[...], other_ref[...]]), work_ref, first_ref)


def second_pass_kernel(kept_ref, other_ref, first_ref, grads_ref, maps_ref, held_ref, work_ref, second_ref, sem):
    rank = first_ref.shape[0]
    held = pltpu.make_async_copy(grads_ref, held_ref, sem)
    held.start()
    first = [
        lax.dot_general(half[...], first_ref[...], LANES_BY_LANES, precision=HIGHEST, preferred_element_type=F32)
        for half in (kept_ref, other_ref)
    ]
    inverse_factor(gram_of(first), work_ref, second_ref)
    both = jnp.dot(second_ref[...], first_ref[...], precision=HIGHEST, preferred_element_type=F32)
    maps_ref[:rank, :] = both
    maps_ref[rank:, :] = lax.dot_general(both, both, ROWS_BY_ROWS, precision=HIGHEST, preferred_element_type=F32)
    held.wait()


def first_pass(power):
    square = (power[0].shape[1],) * 2
    return pl.pallas_call(
        first_pass_kernel,
        out_shape=jax.ShapeDtypeStruct(square, F32),
        in_specs=[IN_VMEM, IN_VMEM],
        out_specs=IN_VMEM,
        scratch_shapes=[pltpu.VMEM(square, F32)],
        compiler_params=pltpu.CompilerParams(vmem_limit_bytes=32 << 20),
        cost_estimate=QR_COST,
    )(*power)


def second_pass(power, first, grads):
    square = first.shape
    return pl.pallas_call(
        second_pass_kernel,
        out_shape=(
            jax.ShapeDtypeStruct((2 * square[0], square[1]), F32),
            jax.ShapeDtypeStruct(grads.shape, grads.dtype),
        ),
        in_specs=[IN_VMEM] * 3 + [IN_HBM],
        out_specs=(IN_VMEM, IN_VMEM),
        scratch_shapes=[pltpu.VMEM(square, F32)] * 2 + [pltpu.SemaphoreType.DMA],
        compiler_params=pltpu.CompilerParams(vmem_limit_bytes=32 << 20),
        cost_estimate=QR_COST,
    )(*power, first, in_hbm(grads))


def power_by_merged(power, grads, errors):
    rank, cols = power.shape[1], grads.shape[1]
    split = jnp.concatenate(pieces(power, 2), axis=1)
    both = jnp.concatenate([grads, errors], axis=1)
    products = lax.dot_general(split, both, ROWS_BY_ROWS, preferred_element_type=F32)
    products = products[:, :cols] + products[:, cols:]
    return products[:rank, :] + products[rank:, :]


def kept_factor_kernel(half_ref, grads_ref, errors_ref, power_ref, terms_ref, other_ref, own_e, sem, other_sem):
    count = power_ref.shape[0]
    rows = half_rows(half_ref[0], count)
    own = pltpu.make_async_copy(errors_ref.at[rows], own_e, sem)
    other = pltpu.make_async_copy(errors_ref.at[half_rows(1 - half_ref[0], count)], other_ref, other_sem)
    own.start()
    other.start()
    own.wait()
    terms_ref[...] = power_by_merged(power_ref[...], grads_ref[rows, :], own_e[...])
    other.wait()


def other_factor_kernel(half_ref, grads_ref, errors_ref, power_ref, before_ref, terms_ref):
    rows = half_rows(1 - half_ref[0], power_ref.shape[0])
    terms_ref[...] = before_ref[...] + power_by_merged(power_ref[...], grads_ref[rows, :], errors_ref[...])


def kept_factor_terms(grads, errors, power, half):
    rows, rank = power.shape
    cols = grads.shape[1]
    return pl.pallas_call(
        kept_factor_kernel,
        out_shape=(jax.ShapeDtypeStruct((rank, cols), F32), jax.ShapeDtypeStruct((rows, cols), BF16)),
        in_specs=[IN_SMEM, IN_VMEM, IN_HBM, IN_VMEM],
        out_specs=(IN_VMEM, IN_VMEM),
        scratch_shapes=[pltpu.VMEM((rows, cols), BF16), pltpu.SemaphoreType.DMA, pltpu.SemaphoreType.DMA],
        compiler_params=pltpu.CompilerParams(vmem_limit_bytes=32 << 20),
        cost_estimate=HALF_COST,
    )(half, grads, in_hbm(errors), power)


def other_factor_terms(grads, other_errors, power, before, half):
    return pl.pallas_call(
        other_factor_kernel,
        out_shape=jax.ShapeDtypeStruct(before.shape, F32),
        in_specs=[IN_SMEM] + [IN_VMEM] * 4,
        out_specs=IN_VMEM,
        compiler_params=pltpu.CompilerParams(vmem_limit_bytes=32 << 20),
        cost_estimate=HALF_COST,
    )(half, grads, other_errors, power, before)


def output_kernel(replicas, place_ref, grads_ref, errors_ref, kept_ref, other_ref, maps_ref, terms_ref,
                  avg_ref, new_ref, q_ref, held_e, held_new, held_avg, held_q, sems, out_sems, avg_sem, q_sem):
    rank = kept_ref.shape[1]
    count = kept_ref.shape[0]
    share = avg_ref.shape[0]
    kept_half, own = place_ref[0], place_ref[1]
    starts = [kept_half * count, (1 - kept_half) * count]
    wait = load((errors_ref,), (held_e,), sems, starts, count)
    writes = []

    def write(held, out, sem):
        writes.append(pltpu.make_async_copy(held, out, sem))
        writes[-1].start()

    def left(values):
        high, low = pieces(values, 2)
        return jnp.concatenate([high, high, low], axis=1)

    def right(values):
        high, low = pieces(values, 2)
        return jnp.concatenate([high, low, high], axis=0)

    def product(values, stacked):
        return jnp.dot(left(values), stacked, preferred_element_type=F32)

    terms = right(terms_ref[...] * (1.0 / replicas))
    mapped = right(product(maps_ref[rank:, :], terms))
    for k, power_ref in enumerate((kept_ref, other_ref)):
        wait(k)
        for part in range(PIECES):
            size = count // PIECES
            piece = slice(part * size, (part + 1) * size)
            held = pl.ds(k * count + part * size, size)
            rows = pl.ds(pl.multiple_of(starts[k] + part * size, size), size)
            merged = grads_ref[rows, :].astype(F32) + held_e[held, :].astype(F32)
            held_new[held, :] = (merged - product(power_ref[piece, :], mapped)).astype(BF16)
            write(held_new.at[held], new_ref.at[rows], out_sems.at[k * PIECES + part])
        if k == 0:
            per_half = count // share
            rows = pl.ds(pl.multiple_of(lax.rem(own, per_half) * share, share), share)
            here = jnp.broadcast_to(own // per_half == kept_half, (share, rank))
            held_avg[...] = product(jnp.where(here, kept_ref[rows, :], other_ref[rows, :]), mapped).astype(BF16)
            write(held_avg, avg_ref, avg_sem)
            held_q[...] = product(maps_ref[:rank, :], terms).T
            write(held_q, q_ref, q_sem)
    for copy in writes:
        copy.wait()


def outputs(grads, errors, power, maps, terms, replicas, place):
    rows, cols = grads.shape
    rank = power[0].shape[1]
    share = rows // replicas
    return pl.pallas_call(
        functools.partial(output_kernel, replicas),
        in_specs=[IN_SMEM, IN_VMEM, IN_HBM] + [IN_VMEM] * 4,
        out_specs=(IN_HBM, IN_HBM, IN_HBM),
        out_shape=(
            jax.ShapeDtypeStruct((share, cols), BF16),
            jax.ShapeDtypeStruct((rows, cols), BF16),
            jax.ShapeDtypeStruct((cols, rank), F32),
        ),
        scratch_shapes=[
            pltpu.VMEM((rows, cols), BF16),
            pltpu.VMEM((rows, cols), BF16),
            pltpu.VMEM((share, cols), BF16),
            pltpu.VMEM((cols, rank), F32),
            pltpu.SemaphoreType.DMA((2, 1)),
            pltpu.SemaphoreType.DMA((2 * PIECES,)),
            pltpu.SemaphoreType.DMA,
            pltpu.SemaphoreType.DMA,
        ],
        compiler_params=pltpu.CompilerParams(vmem_limit_bytes=16 << 20),
    )(place, grads, in_hbm(errors), *power, maps, terms)


def exchange(values, axes, groups):
    return lax.all_to_all(values, axes, 0, 0, axis_index_groups=groups, tiled=True)


def members(axes, groups):
    return lax.axis_size(axes) if groups is None else len(groups[0])


def scatter_sum(values, axes, groups=None):
    count = members(axes, groups)
    shares = exchange(values, axes, groups)
    return shares.reshape(count, values.shape[0] // count, values.shape[1]).sum(axis=0)


def gather(values, axes, groups=None):
    copies = jnp.broadcast_to(values[None], (members(axes, groups), *values.shape)).reshape(-1, values.shape[1])
    return exchange(copies, axes, groups)


def exchange_sum(values, axes, groups):
    return gather(values, axes, groups).reshape(members(axes, groups), *values.shape).sum(axis=0)


def z_groups(length, width):
    blocks = length // NEAR

    def device(block, share, y):
        turn = NEAR // 2 if 2 * block >= blocks else 0
        return (block * NEAR + (share + turn) % NEAR) * width + y

    shares = [(share, y) for share in range(NEAR) for y in range(width)]
    near = [[device(block, *share) for share in shares] for block in range(blocks)]
    far = [[device(block, *share) for block in range(blocks)] for share in shares]
    return near, far


def swap(values):
    return lax.ppermute(values, "core", [(0, 1), (1, 0)])


def body(grads, errors, q_init):
    replicas = lax.axis_size(DP)
    half = lax.axis_index("core").reshape(1)
    sent, own_grads = sent_power_terms(grads, errors, q_init, half)
    received = swap(sent)
    power = kept_power_terms(own_grads, errors, q_init, half) + received

    near, far = z_groups(lax.axis_size("z"), 1)
    power = scatter_sum(power, ("y", "x"))
    power = exchange_sum(power, "z", near)
    power = exchange_sum(power, "z", far)
    power = gather(power, ("y", "x"))
    power = (power, swap(power))

    near, far = z_groups(lax.axis_size("z"), lax.axis_size("y"))
    terms, other_errors = kept_factor_terms(grads, errors, power[0], half)
    terms = other_factor_terms(grads, other_errors, power[1], terms, half)
    first = first_pass(power)
    place = jnp.concatenate([half, lax.axis_index(DP).reshape(1)])
    terms = scatter_sum(terms, DP, near)
    terms, first, place = lax.optimization_barrier((terms, first, place))
    terms = exchange_sum(terms, DP, far)
    terms, first = lax.optimization_barrier((terms, first))
    maps, held_grads = second_pass(power, first, grads)
    terms = gather(terms, DP, near)
    return outputs(held_grads, errors, power, maps, terms, replicas, place)


def solution(mesh):
    fine = Mesh(mesh.devices.reshape(16, 4, 4, 2), ("z", "y", "x", "core"))
    placed = (P(DP, TENSOR), P(DP, TENSOR), P(TENSOR, None))
    return jax.shard_map(
        body,
        mesh=fine,
        in_specs=placed,
        out_specs=(P(DP, TENSOR), P(DP, TENSOR), P(TENSOR, None)),
        check_vma=False,
    )
```
